512 devices in a mesh: row: 16 (over x, y_hi, core), col: 32 (over z, y_lo).
Axes of the slice: x: 4, y: 4 (y_hi: 2, y_lo: 2; y = y_hi * 2 + y_lo), z: 16, core: 2. Of those that a mesh axis runs over, the one named last changes fastest.
Arguments:
- covariance: float32 [16384, 16384], P('row', 'col'), may hold values from -6 to 6
- courant_table: float32 [8, 128], replicated, may hold values from -0.45 to 0.45
- step_wind_rows: int32 [2, 3], replicated, may hold values from 0 to 7
- barriers: int32 [4], replicated, may hold values from 1 to 127
- tracer_a_mixing: float32 [128, 128, 128], P('row'), may hold values from -1 to 2
- tracer_b_mixing: float32 [128, 128, 128], P('col'), may hold values from -1 to 2
Outputs:
- forecast: float32 [16384, 16384], P('col', 'row')
The draws below stay inside these ranges and needn't reach their ends.
All inputs are finite; a program needn't handle non-finite values.
Results may differ from the reference program's by a relative error of at most 0.00016.
Values sent between devices are 32-bit elements; how exact they have to be, the bound alone decides.
No kernel may reach another device: no remote copies, remote signals or barrier semaphores. Data moves between devices by JAX's collectives and lax.ppermute only.
A program may use at most 64 MiB of HBM per device.

```python
import jax
import jax.numpy as jnp
from jax import lax

LAT = 128
LEV = 128
STEPS = 3
WINDS = 8
BARRIERS = 4
STATES = 16384


def mixing_draw(key):
    noise = jax.random.normal(key, (LAT, LEV, LEV), jnp.float32)
    return jnp.eye(LEV, dtype=jnp.float32)[None] + 0.35 * noise / jnp.sqrt(jnp.float32(LEV))


def draw_tracer_a_mixing(key, part):
    return mixing_draw(jax.random.fold_in(key, 11))


def draw_tracer_b_mixing(key, part):
    return mixing_draw(jax.random.fold_in(key, 23))


def plant(drawn, stream_key, least, largest):
    longest = drawn.shape.index(max(drawn.shape))
    spots = []
    for shift in (0, 1):
        where = [jax.random.randint(jax.random.fold_in(stream_key, axis), (), 0, length) for axis, length in enumerate(drawn.shape)]
        where[longest] = (where[longest] + shift) % drawn.shape[longest]
        spots.append(tuple(where))
    return drawn.at[spots[0]].set(least).at[spots[1]].set(largest)


def block_levels(key, shape, shards, least, high):
    gain, own = 1.0, jax.random.fold_in(key, 6)
    for position, shards_of in shards:
        heights = jnp.exp(jax.random.uniform(jax.random.fold_in(own, position), (shards_of,), jnp.float32, least / len(shards), high / len(shards)))
        gain = gain * jnp.repeat(heights, shape[position] // shards_of).reshape([-1 if axis == position else 1 for axis in range(len(shape))])
    return gain


def bell_draw(key, dims, scale, most, pieces=(), kind=jnp.bfloat16):
    values = jax.random.normal(key, dims, jnp.float32) * scale
    if len(pieces) > 0:
        values = block_levels(key, dims, pieces, -0.22, 0.18) * values
    return jnp.clip(values, min=-most, max=most).astype(kind)


def setup_inputs(seed: int = 0) -> dict:
    streams_of = jax.random.split(jax.random.key(seed), 7)
    covariance = bell_draw(streams_of[0], (STATES, STATES), 1.0, 6.0, ((0, 16), (1, 32)), jnp.float32)
    courant_table = jnp.clip(jax.random.uniform(streams_of[1], (WINDS, LAT), jnp.float32, -0.45, 0.45), -0.45, 0.45)
    step_wind_rows = plant(jax.random.randint(streams_of[2], (2, STEPS), 0, WINDS), jax.random.fold_in(streams_of[2], 1), 0, WINDS - 1).astype(jnp.int32)
    barriers = plant(jax.random.randint(streams_of[3], (BARRIERS,), 1, LAT), jax.random.fold_in(streams_of[3], 1), 1, LAT - 1).astype(jnp.int32)
    tracer_a_mixing = draw_tracer_a_mixing(jax.random.fold_in(streams_of[6], 71), 0)
    tracer_b_mixing = draw_tracer_b_mixing(jax.random.fold_in(streams_of[6], 71), 0)
    return {"covariance": covariance, "courant_table": courant_table, "step_wind_rows": step_wind_rows, "barriers": barriers, "tracer_a_mixing": tracer_a_mixing, "tracer_b_mixing": tracer_b_mixing}


def advance(extended, vertical_mixer, table_row, barriers, anchor, lat_count):
    edges = anchor + lax.iota(jnp.int32, lat_count + 1)
    inside = (edges >= 1) & (edges <= LAT - 1)
    courant = jnp.take(table_row, jnp.clip(edges, 0, LAT - 1).astype(jnp.int32))
    blocked = jnp.any(edges[:, None] == barriers[None, :], axis=1)
    courant = jnp.where(inside, courant * jnp.where(blocked, 0.25, 1.0), 0.0).astype(jnp.float32)
    spread = jnp.where(inside, 0.15, 0.0).astype(jnp.float32)[:, None, None]
    forward = jnp.maximum(courant, 0.0)[:, None, None]
    backward = jnp.maximum(-courant, 0.0)[:, None, None]
    fluxes = forward * extended[:-1] - backward * extended[1:] + spread * (extended[:-1] - extended[1:])
    shifted = extended[1:-1] + fluxes[:-1] - fluxes[1:]
    return jnp.einsum("lij,ljc->lic", vertical_mixer, shifted, precision=lax.Precision.HIGHEST)


def predicted_columns(latitude_block, vertical_mixer, courant_table, rows_per_step, barriers):
    field = latitude_block.reshape(LAT, LEV, latitude_block.shape[1])
    for moment in range(STEPS):
        padded = jnp.pad(field, ((1, 1), (0, 0), (0, 0)))
        field = advance(padded, vertical_mixer, courant_table[rows_per_step[moment]], barriers, 0, LAT)
    return field.reshape(LAT * LEV, latitude_block.shape[1])


def reference(covariance, courant_table, step_wind_rows, barriers, tracer_a_mixing, tracer_b_mixing):
    covered_columns = LEV * 4
    blocks = LAT // 4
    states = LAT * LEV
    start_shifts = jnp.arange(blocks, dtype=jnp.int32)
    stepped_forward = lax.map(lambda start_shift: predicted_columns(lax.dynamic_slice_in_dim(covariance, start_shift * covered_columns, covered_columns, 1), tracer_a_mixing, courant_table, step_wind_rows[0], barriers), start_shifts)
    reversed_order = stepped_forward.transpose(0, 2, 1).reshape(states, states)
    completed_result = lax.map(lambda start_shift: predicted_columns(lax.dynamic_slice_in_dim(reversed_order, start_shift * covered_columns, covered_columns, 1), tracer_b_mixing, courant_table, step_wind_rows[1], barriers), start_shifts)
    return completed_result.transpose(1, 0, 2).reshape(states, states)
```

```python
import functools
import itertools

import jax
import jax.numpy as jnp
from jax import lax
from jax.experimental import pallas as pl
from jax.experimental.pallas import tpu as pltpu
from jax.sharding import PartitionSpec as P

LAT = 128
LEV = 128
STEPS = 3
SPREAD = 0.15
WINDOW = 14
F32, BF16 = jnp.float32, jnp.bfloat16
AXES = ("row", "col")
ANY = pl.BlockSpec(memory_space=pl.ANY)
SMEM = pl.BlockSpec(memory_space=pltpu.SMEM)
VMEM = pl.BlockSpec(memory_space=pltpu.VMEM)


def pairs(move, x_size, z_size):
    number = lambda x, h, k, z, l: ((x * 2 + h) * 2 + k) * (2 * z_size) + z * 2 + l
    listed = []
    for x, h, k, z, l in itertools.product(range(x_size), range(2), range(2), range(z_size), range(2)):
        to = move(x, h, k, z, l)
        if to is not None and 0 <= to[0] < x_size and 0 <= to[3] < z_size:
            listed.append((number(x, h, k, z, l), number(*to)))
    return listed


def row_shift(x, h, k, by):
    at = (x * 2 + h) * 2 + k + by
    return at // 4, (at // 2) % 2, at % 2


def swap_y(x, h, k, z, l):
    return x, h, k, z, 1 - l


def near_z(x, h, k, z, l):
    return x, h, k, z + (1 if l else -1), l


def far_z(x, h, k, z, l):
    return x, h, k, z + (-1 if l else 1), l


def mats_group(x, h, k, z, l):
    return x, 1 - h, k, z, 1 - l


def mats_far(x, h, k, z, l):
    return x, 1 - h, k, z + (1 if l else -1), 1 - l


def mats_row(by, x, h, k, z, l):
    tx, th, tk = row_shift(x, h, k, by)
    return tx, th, tk, z, (l if (tx, th) == (x, h) else 1 - l)


def halo_same(x, h, k, z, l):
    return *row_shift(x, h, k, 1 if l else -1), z, l


def halo_cross(x, h, k, z, l):
    tx, th, tk = row_shift(x, h, k, 1 if l else -1)
    return None if (tx, th) == (x, h) else (tx, th, tk, z, 1 - l)


def relay_core(x, h, k, z, l):
    return (x, h, 1 - k, z, l) if k == l else None


def side():
    return lax.rem(lax.axis_index("col"), 2)


def turned(l, q, count):
    return jnp.where(l == 1, q, count - 1 - q)


def rows_of(l, chunk):
    return l * 768 if chunk == 0 else 256 + l * 256


def run_copies(copies, sems):
    started = []
    for i, (src, dst) in enumerate(copies):
        copy = pltpu.make_async_copy(src, dst, sems.at[i])
        copy.start()
        started.append(copy)
    for copy in started:
        copy.wait()


def lanes(start):
    return pl.ds(pl.multiple_of(start * LEV, LEV), LEV)


def rows(start, size):
    return pl.ds(pl.multiple_of(start, LEV), size)


def pack_first(cov, out, sems):
    l = side()
    at = rows_of(1 - l, 0)
    run_copies([(cov.at[rows(at, 256), lanes(l + i)], out.at[i]) for i in range(3)], sems)


def pack_rest(cov, mix, second, single, near, edge, sems):
    l = side()
    at = rows_of(1 - l, 1)
    copies = [(cov.at[rows(at, 256), lanes(l + i)], second.at[i]) for i in range(3)]
    for c in range(2):
        copies.append((cov.at[rows(rows_of(1 - l, c), 256), lanes(3 - 3 * l)], single.at[c]))
        for i in range(3):
            copies.append((cov.at[rows(rows_of(l, c), 256), lanes(l + i)], near.at[3 * c + i]))
    for m in range(2):
        copies.append((mix.at[2 * l + m], near.at[6, pl.ds(m * LEV, LEV)]))
        copies.append((mix.at[2 * l + m], edge.at[m]))
    run_copies(copies, sems)


def write_coefficients(l, base, tracer, table, winds, barriers, coef, flow):
    def interface(step, n):
        g = base + n - 3
        inside = (g >= 1) & (g <= LAT - 1)
        c = table[winds[tracer, step], jnp.clip(g, 0, LAT - 1)]
        blocked = barriers[0] == g
        for b in range(1, 4):
            blocked = blocked | (barriers[b] == g)
        c = c * jnp.where(blocked, 0.25, 1.0)
        flow[0, n] = jnp.where(inside, jnp.maximum(c, 0.0) + SPREAD, 0.0)
        flow[1, n] = jnp.where(inside, jnp.maximum(-c, 0.0) + SPREAD, 0.0)

    for step in range(STEPS):
        lax.fori_loop(0, WINDOW + 1, lambda n, _: interface(step, n), None)

        def place(p, _):
            n = turned(l, p, WINDOW)
            below, above = flow[0, n], flow[1, n + 1]
            coef[step * 48 + p] = jnp.where(l == 1, below, above)
            coef[step * 48 + 16 + p] = 1.0 - flow[1, n] - flow[0, n + 1]
            coef[step * 48 + 32 + p] = jnp.where(l == 1, above, below)

        lax.fori_loop(0, WINDOW, place, None)


def write_weight(weights, at, mixer):
    turned_mixer = mixer.T
    high = turned_mixer.astype(BF16)
    low = (turned_mixer - high.astype(F32)).astype(BF16)
    for half in range(2):
        weights[at, half * LEV : (half + 1) * LEV, :LEV] = high
        weights[at, half * LEV : (half + 1) * LEV, LEV:] = low


def prepare_b(table, winds, barriers, near, group, own, far, weights, coef, flow):
    l = side()
    base = lax.axis_index("col") // 2 * 8
    write_coefficients(l, base, 1, table, winds, barriers, coef, flow)
    for q in range(2):
        m = turned(l, q, 2)
        write_weight(weights, q, near[0, pl.ds(pl.multiple_of(m * LEV, LEV), LEV), :])
        write_weight(weights, 10 + q, far[m])
    for q in range(4):
        b = turned(l, q, 4)
        write_weight(weights, 2 + q, group[b])
        write_weight(weights, 6 + q, own[b])


def prepare_a(table, winds, barriers, own, before, after, weights, coef, flow):
    l = side()
    base = lax.axis_index("row") * 8
    write_coefficients(l, base, 0, table, winds, barriers, coef, flow)
    for q in range(8):
        write_weight(weights, 2 + q, own[turned(l, q, 8)])
    for q in range(2):
        write_weight(weights, q, jnp.where(l == 1, before[q], after[1 - q]))
        write_weight(weights, 10 + q, jnp.where(l == 1, after[q], before[1 - q]))


def step_latitude(step, p, source, weights, coef):
    y = (
        coef[step * 48 + p] * source[p - 1]
        + coef[step * 48 + 16 + p] * source[p]
        + coef[step * 48 + 32 + p] * source[p + 1]
    )
    high = y.astype(BF16)
    low = (y - high.astype(F32)).astype(BF16)
    both = jnp.dot(
        jnp.concatenate([high, low], axis=1), weights[p - 1], preferred_element_type=F32
    )
    return both[:, :LEV] + both[:, LEV:]


def first_steps(window, other, weights, coef):
    def first(p, _):
        other[p] = step_latitude(0, p, window, weights, coef)

    def second(p, _):
        window[p] = step_latitude(1, p, other, weights, coef)

    lax.fori_loop(1, WINDOW - 1, first, None)
    lax.fori_loop(2, WINDOW - 2, second, None)


def sweep_b(chunk, *refs):
    if chunk == 0:
        coef, weights, cov, pair, single, near, far, kept, sent, window, other, sems = refs
    else:
        (coef, weights, cov, pair, single, near, far, kept_before, sent_before,
         kept, sent, same, cross, window, other, sems, late) = refs
    l = side()
    copies = []
    for q in range(3):
        t = turned(l, q, 3)
        copies.append((near.at[3 * chunk + t], window.at[q]))
        copies.append((pair.at[t], window.at[3 + q]))
        copies.append((far.at[t], window.at[11 + q]))
    copies.append((single.at[chunk], window.at[6]))
    for q in range(4):
        copies.append((cov.at[rows(rows_of(l, chunk), 256), lanes(turned(l, q, 4))], window.at[7 + q]))
    run_copies(copies, sems)
    first_steps(window, other, weights, coef)

    def finish(p, target, q):
        z = step_latitude(2, p, window, weights, coef)
        b = turned(l, q, 4)
        for i in range(2):
            u = turned(l, i, 2)
            target[u, rows(b * LEV, LEV), :] = z[i * LEV : (i + 1) * LEV].T

    lax.fori_loop(0, 4, lambda q, _: finish(3 + q, sent, q), None)
    lax.fori_loop(0, 4, lambda q, _: finish(7 + q, kept, q), None)
    if chunk == 1:
        run_copies(
            [
                (kept_before, same.at[pl.ds(1, 2)]),
                (sent_before, cross.at[pl.ds(1, 2)]),
                (kept.at[1], same.at[0]),
                (sent.at[1], cross.at[0]),
            ],
            late,
        )


def sweep_a(coef, weights, kept_0, kept_1, got_0, got_1, same, cross, relay_0, relay_1, out,
            window, other, sems):
    l = side()
    k = lax.rem(lax.axis_index("row"), 2)
    copies = [(same.at[q], window.at[q]) for q in range(3)]
    for u in range(2):
        copies.append((kept_1.at[u], window.at[7 + u]))
        copies.append((kept_0.at[u], window.at[9 + u]))
        copies.append((got_0.at[u], window.at[4 - u]))
        copies.append((got_1.at[u], window.at[6 - u]))
    across = [(cross.at[q], window.at[13 - q]) for q in range(3)]
    inside = [(relay_1.at[1], window.at[13])] + [(relay_0.at[u], window.at[12 - u]) for u in range(2)]

    @pl.when(k == l)
    def _():
        run_copies(across, sems)

    @pl.when(k != l)
    def _():
        run_copies(inside, sems)

    run_copies(copies, sems)
    first_steps(window, other, weights, coef)

    def finish(p, _):
        out[:, lanes(turned(l, p - 3, 8))] = step_latitude(2, p, window, weights, coef)

    lax.fori_loop(3, WINDOW - 3, finish, None)


def call(kernel, outs, in_specs, out_specs, scratch, flops, name):
    return pl.pallas_call(
        kernel,
        out_shape=outs,
        in_specs=in_specs,
        out_specs=out_specs,
        scratch_shapes=scratch,
        compiler_params=pltpu.CompilerParams(vmem_limit_bytes=40 * 1024 * 1024),
        cost_estimate=pl.CostEstimate(flops=flops, bytes_accessed=2**21, transcendentals=0),
        name=name,
    )


def shaped(*dims, dtype=F32):
    return jax.ShapeDtypeStruct(dims, dtype)


def per_device(x_size, z_size, covariance, table, winds, barriers, mix_a, mix_b):
    send = lambda value, move: lax.ppermute(value, AXES, pairs(move, x_size, z_size))
    dma = lambda n: pltpu.SemaphoreType.DMA((n,))

    out_0 = call(pack_first, shaped(3, 256, LEV), [ANY], ANY, [dma(3)], 0, "pack_first")(covariance)
    pair_0 = send(out_0, swap_y)
    out_1, out_single, out_near, edge = call(
        pack_rest,
        (shaped(3, 256, LEV), shaped(2, 256, LEV), shaped(7, 256, LEV), shaped(2, LEV, LEV)),
        [ANY, ANY], (ANY,) * 4, [dma(15)], 0, "pack_rest",
    )(covariance, mix_b)
    near = send(out_near, near_z)
    pair_1 = send(out_1, swap_y)
    far_0 = send(pair_0, far_z)
    single = send(out_single, swap_y)
    far_1 = send(pair_1, far_z)
    group = send(mix_b, mats_group)
    edge_far = send(edge, mats_far)
    before = send(mix_a[6:8], functools.partial(mats_row, 1))
    after = send(mix_a[0:2], functools.partial(mats_row, -1))

    prep_outs = (shaped(12, 256, 256, dtype=BF16), shaped(144))
    prep_scratch = [pltpu.SMEM((2, 16), F32)]
    weights_b, coef_b = call(
        prepare_b, prep_outs, [SMEM] * 3 + [VMEM] * 4, (VMEM, SMEM), prep_scratch, 10**8, "prepare_b"
    )(table, winds, barriers, near[6:7], group, mix_b, edge_far)
    weights_a, coef_a = call(
        prepare_a, prep_outs, [SMEM] * 3 + [VMEM] * 3, (VMEM, SMEM), prep_scratch, 10**8, "prepare_a"
    )(table, winds, barriers, mix_a, before, after)

    block = shaped(2, 512, LEV)
    field = pltpu.VMEM((WINDOW, 256, LEV), F32)
    kept_0, sent_0 = call(
        functools.partial(sweep_b, 0), (block,) * 2, [SMEM, VMEM] + [ANY] * 5, (VMEM,) * 2,
        [field, field, dma(14)], 2 * 10**9, "sweep_b0",
    )(coef_b, weights_b, covariance, pair_0, single, near, far_0)
    got_0 = send(sent_0, swap_y)
    kept_1, sent_1, out_same, out_cross = call(
        functools.partial(sweep_b, 1), (block,) * 2 + (shaped(3, 512, LEV),) * 2,
        [SMEM, VMEM] + [ANY] * 7, (VMEM, VMEM, ANY, ANY),
        [field, field, dma(14), dma(4)], 2 * 10**9, "sweep_b1",
    )(coef_b, weights_b, covariance, pair_1, single, near, far_1, kept_0, sent_0)
    got_1 = send(sent_1, swap_y)
    same = send(out_same, halo_same)
    cross = send(out_cross, halo_cross)
    relay_0 = send(got_0, relay_core)
    relay_1 = send(got_1, relay_core)

    field = pltpu.VMEM((WINDOW, 512, LEV), F32)
    return call(
        sweep_a, shaped(512, 1024), [SMEM, VMEM] + [ANY] * 8, VMEM, [field, field, dma(11)],
        4 * 10**9, "sweep_a",
    )(coef_a, weights_a, kept_0, kept_1, got_0, got_1, same, cross, relay_0, relay_1)


def solution(mesh):
    placed = (P("row", "col"), P(), P(), P(), P("row", None, None), P("col", None, None))
    return jax.shard_map(
        functools.partial(per_device, mesh.shape["row"] // 4, mesh.shape["col"] // 2),
        mesh=mesh, in_specs=placed, out_specs=P("col", "row"), check_vma=False,
    )
```

```python
import functools
import itertools

import jax
import jax.numpy as jnp
from jax import lax
from jax.experimental import pallas as pl
from jax.experimental.pallas import tpu as pltpu
from jax.sharding import PartitionSpec as P

LAT = 128
LEV = 128
STEPS = 3
SPREAD = 0.15
WINDOW = 14
F32, BF16 = jnp.float32, jnp.bfloat16
COST = 4 * 10**9
AXES = ("row", "col")
ANY = pl.BlockSpec(memory_space=pl.ANY)
SMEM = pl.BlockSpec(memory_space=pltpu.SMEM)
VMEM = pl.BlockSpec(memory_space=pltpu.VMEM)


def pairs(move, x_size, z_size):
    number = lambda x, h, k, z, l: ((x * 2 + h) * 2 + k) * (2 * z_size) + z * 2 + l
    listed = []
    for x, h, k, z, l in itertools.product(range(x_size), range(2), range(2), range(z_size), range(2)):
        to = move(x, h, k, z, l)
        if to is not None and 0 <= to[0] < x_size and 0 <= to[3] < z_size:
            listed.append((number(x, h, k, z, l), number(*to)))
    return listed


def row_shift(x, h, k, by):
    at = (x * 2 + h) * 2 + k + by
    return at // 4, (at // 2) % 2, at % 2


def swap_y(x, h, k, z, l):
    return x, h, k, z, 1 - l


def near_z(x, h, k, z, l):
    return x, h, k, z + (1 if l else -1), l


def far_z(x, h, k, z, l):
    return x, h, k, z + (-1 if l else 1), l


def mats_across(size, x, h, k, z, l):
    tx, th, tk = row_shift(x, h, k, 1 if k else -1)
    return tx % size, th, tk, z, 1 - l


def mats_core(x, h, k, z, l):
    return x, h, 1 - k, z, l


def halo_same(x, h, k, z, l):
    return *row_shift(x, h, k, 1 if l else -1), z, l


def halo_cross(x, h, k, z, l):
    tx, th, tk = row_shift(x, h, k, 1 if l else -1)
    return None if (tx, th) == (x, h) else (tx, th, tk, z, 1 - l)


def halo_flip(x, h, k, z, l):
    return *row_shift(x, h, k, 1 if l else -1), z, 1 - l


def relay_core(x, h, k, z, l):
    return (x, h, 1 - k, z, l) if k == l else None


def side():
    return lax.rem(lax.axis_index("col"), 2)


def turned(l, q, count):
    return jnp.where(l == 1, q, count - 1 - q)


def rows_of(l, chunk):
    return l * 768 if chunk == 0 else 256 + l * 256


def run_copies(copies, sems):
    started = []
    for i, (src, dst) in enumerate(copies):
        copy = pltpu.make_async_copy(src, dst, sems.at[i])
        copy.start()
        started.append(copy)
    for copy in started:
        copy.wait()


def lanes(start):
    return pl.ds(pl.multiple_of(start * LEV, LEV), LEV)


def rows(start, size):
    return pl.ds(pl.multiple_of(start, LEV), size)


def pack_first(cov, out, sems):
    l = side()
    at = rows_of(1 - l, 0)
    copies = [(cov.at[rows(at, 256), lanes(l + i)], out.at[i]) for i in range(3)]
    run_copies(copies + [(cov.at[rows(at, 256), lanes(3 - 3 * l)], out.at[3])], sems)


def pack_rest(cov, mix_a, mix_b, second, near, across, core, sems):
    l = side()
    k = lax.rem(lax.axis_index("row"), 2)
    at = rows_of(1 - l, 1)
    copies = [(mix_b, across.at[pl.ds(0, 4)])]
    copies.append((mix_a.at[pl.ds(6 * k, 2)], across.at[pl.ds(4, 2)]))
    copies.append((mix_a.at[pl.ds(6 - 6 * k, 2)], core))
    copies += [(cov.at[rows(at, 256), lanes(l + i)], second.at[i]) for i in range(3)]
    copies.append((cov.at[rows(at, 256), lanes(3 - 3 * l)], second.at[3]))
    for c in range(2):
        for i in range(3):
            copies.append((cov.at[rows(rows_of(l, c), 256), lanes(l + i)], near.at[3 * c + i]))
    for m in range(2):
        copies.append((mix_b.at[2 * l + m], near.at[6, pl.ds(m * LEV, LEV)]))
    run_copies(copies, sems)


def pack_far(pair, across, out, sems):
    l = side()
    copies = [(pair.at[pl.ds(0, 3)], out.at[pl.ds(0, 3)])]
    for m in range(2):
        copies.append((across.at[2 - 2 * l + m], out.at[3, pl.ds(m * LEV, LEV)]))
    run_copies(copies, sems)


def write_coefficients(l, base, tracer, table, winds, barriers, coef, flow):
    def interface(step, n):
        g = base + n - 3
        inside = (g >= 1) & (g <= LAT - 1)
        c = table[winds[tracer, step], jnp.clip(g, 0, LAT - 1)]
        blocked = barriers[0] == g
        for b in range(1, 4):
            blocked = blocked | (barriers[b] == g)
        c = c * jnp.where(blocked, 0.25, 1.0)
        flow[0, n] = jnp.where(inside, jnp.maximum(c, 0.0) + SPREAD, 0.0)
        flow[1, n] = jnp.where(inside, jnp.maximum(-c, 0.0) + SPREAD, 0.0)

    for step in range(STEPS):
        lax.fori_loop(0, WINDOW + 1, lambda n, _: interface(step, n), None)

        def place(p, _):
            n = turned(l, p, WINDOW)
            below, above = flow[0, n], flow[1, n + 1]
            coef[step * 48 + p] = jnp.where(l == 1, below, above)
            coef[step * 48 + 16 + p] = 1.0 - flow[1, n] - flow[0, n + 1]
            coef[step * 48 + 32 + p] = jnp.where(l == 1, above, below)

        lax.fori_loop(0, WINDOW, place, None)


def write_weight(weights, at, mixer):
    turned_mixer = mixer.T
    high = turned_mixer.astype(BF16)
    low = (turned_mixer - high.astype(F32)).astype(BF16)
    for half in range(2):
        weights[at, half * LEV : (half + 1) * LEV, :LEV] = high
        weights[at, half * LEV : (half + 1) * LEV, LEV:] = low


def prepare_b(table, winds, barriers, across, own, weights, coef, flow):
    l = side()
    base = lax.axis_index("col") // 2 * 8
    write_coefficients(l, base, 1, table, winds, barriers, coef, flow)
    for q in range(4):
        b = turned(l, q, 4)
        write_weight(weights, q, across[b])
        write_weight(weights, 4 + q, own[b])


def prepare_a(table, winds, barriers, own, across, core, weights, ends, coef, flow):
    l = side()
    k = lax.rem(lax.axis_index("row"), 2)
    base = lax.axis_index("row") * 8
    write_coefficients(l, base, 0, table, winds, barriers, coef, flow)
    for q in range(8):
        write_weight(weights, q, own[turned(l, q, 8)])
    for q in range(2):
        m = turned(l, q, 2)
        write_weight(ends, q, jnp.where(k == l, core[m], across[4 + m]))
        write_weight(ends, 2 + q, jnp.where(k == l, across[4 + m], core[m]))


def step_latitude(step, p, source, weights, ends, coef):
    weight = weights[p - 3] if 3 <= p <= 10 else ends[p - 1 if p < 3 else p - 9]
    y = (
        coef[step * 48 + p] * source[p - 1]
        + coef[step * 48 + 16 + p] * source[p]
        + coef[step * 48 + 32 + p] * source[p + 1]
    )
    high = y.astype(BF16)
    low = (y - high.astype(F32)).astype(BF16)
    both = jnp.dot(
        jnp.concatenate([high, low], axis=1), weight, preferred_element_type=F32
    )
    return both[:, :LEV] + both[:, LEV:]


def first_steps(window, other, weights, ends, coef):
    for p in range(1, WINDOW - 1):
        other[p] = step_latitude(0, p, window, weights, ends, coef)
    for p in range(2, WINDOW - 2):
        window[p] = step_latitude(1, p, other, weights, ends, coef)


def sweep_b(chunk, *refs):
    if chunk == 0:
        coef, weights, cov, pair, near, far, kept, sent, ends, window, other, edge, sems = refs
    else:
        (coef, weights, cov, pair, near, far, ends, kept, sent, same, cross, window, other, sems,
         late) = refs
    l = side()
    copies = []
    for q in range(3):
        t = turned(l, q, 3)
        copies.append((near.at[3 * chunk + t], window.at[q]))
        copies.append((pair.at[t], window.at[3 + q]))
        copies.append((far.at[t], window.at[11 + q]))
    copies.append((pair.at[3], window.at[6]))
    for q in range(4):
        copies.append((cov.at[rows(rows_of(l, chunk), 256), lanes(turned(l, q, 4))], window.at[7 + q]))
    if chunk == 0:
        copies += [(near.at[6], edge.at[0]), (far.at[3], edge.at[1])]
    run_copies(copies, sems)
    if chunk == 0:
        for place in range(2):
            for q in range(2):
                m = turned(l, q, 2)
                write_weight(ends, 2 * place + q, edge[place, rows(m * LEV, LEV), :])
    first_steps(window, other, weights, ends, coef)

    def finish(p, target, q):
        z = step_latitude(2, p, window, weights, ends, coef)
        b = turned(l, q, 4)
        for i in range(2):
            u = turned(l, i, 2)
            target[u, rows(b * LEV, LEV), :] = z[i * LEV : (i + 1) * LEV].T

    for q in range(4):
        finish(3 + q, sent, q)
    for q in range(4):
        finish(7 + q, kept, q)
    if chunk == 1:
        run_copies([(kept.at[1], same.at[0]), (sent.at[1], cross.at[0])], late)


def sweep_a(coef, weights, ends, kept_0, kept_1, got_0, got_1, same_0, same_1, cross_0, cross_1, relay, out,
            window, other, sems):
    l = side()
    k = lax.rem(lax.axis_index("row"), 2)
    copies = [(same_1.at[0], window.at[0])] + [(same_0.at[u], window.at[1 + u]) for u in range(2)]
    for u in range(2):
        copies.append((kept_1.at[u], window.at[7 + u]))
        copies.append((kept_0.at[u], window.at[9 + u]))
        copies.append((got_0.at[u], window.at[4 - u]))
        copies.append((got_1.at[u], window.at[6 - u]))
    copies.append((cross_1.at[0], window.at[13]))
    across = [(cross_0.at[u], window.at[12 - u]) for u in range(2)]
    inside = [(relay.at[u], window.at[12 - u]) for u in range(2)]

    @pl.when(k == l)
    def _():
        run_copies(across, sems)

    @pl.when(k != l)
    def _():
        run_copies(inside, sems)

    run_copies(copies, sems)
    first_steps(window, other, weights, ends, coef)

    for p in range(3, WINDOW - 3):
        out[:, lanes(turned(l, p - 3, 8))] = step_latitude(2, p, window, weights, ends, coef)


def call(kernel, outs, in_specs, out_specs, scratch, flops, name):
    return pl.pallas_call(
        kernel,
        out_shape=outs,
        in_specs=in_specs,
        out_specs=out_specs,
        scratch_shapes=scratch,
        compiler_params=pltpu.CompilerParams(vmem_limit_bytes=40 * 1024 * 1024),
        cost_estimate=pl.CostEstimate(flops=flops, bytes_accessed=2**10, transcendentals=0),
        name=name,
    )


def shaped(*dims, dtype=F32):
    return jax.ShapeDtypeStruct(dims, dtype)


def per_device(x_size, z_size, covariance, table, winds, barriers, mix_a, mix_b):
    send = lambda value, move: lax.ppermute(value, AXES, pairs(move, x_size, z_size))
    dma = lambda n: pltpu.SemaphoreType.DMA((n,))

    out_0 = call(pack_first, shaped(4, 256, LEV), [ANY], ANY, [dma(4)], 0, "pack_first")(covariance)
    pair_0 = send(out_0, swap_y)
    covariance, out_0 = lax.optimization_barrier((covariance, out_0))
    pair_0 = send(out_0, swap_y)
    out_1, out_near, out_across, out_core = call(
        pack_rest,
        (shaped(4, 256, LEV), shaped(7, 256, LEV), shaped(6, LEV, LEV), shaped(2, LEV, LEV)),
        [ANY] * 3, (ANY,) * 4, [dma(15)], 0, "pack_rest",
    )(covariance, mix_a, mix_b)
    across = send(out_across, functools.partial(mats_across, x_size))
    near = send(out_near, near_z)
    core = send(out_core, mats_core)
    pair_1 = send(out_1, swap_y)
    across, core = lax.optimization_barrier((across, core))
    out_far = call(pack_far, shaped(4, 256, LEV), [ANY] * 2, ANY, [dma(3)], 0, "pack_far")(pair_0, across)
    far_0 = send(out_far, far_z)
    far_1 = send(pair_1[:3], far_z)

    weight = shaped(8, 256, 256, dtype=BF16)
    ends = shaped(4, 256, 256, dtype=BF16)
    prep_scratch = [pltpu.SMEM((2, 16), F32)]
    weights_b, coef_b = call(
        prepare_b, (weight, shaped(144)), [SMEM] * 3 + [VMEM] * 2, (VMEM, SMEM), prep_scratch, 10**3,
        "prepare_b",
    )(table, winds, barriers, across, mix_b)
    block = shaped(2, 512, LEV)
    field = pltpu.VMEM((WINDOW, 256, LEV), F32)
    kept_0, sent_0, ends_b = call(
        functools.partial(sweep_b, 0), (block, block, ends), [SMEM, VMEM] + [ANY] * 4, (VMEM,) * 3,
        [field, field, pltpu.VMEM((2, 256, LEV), F32), dma(16)], COST, "sweep_b0",
    )(coef_b, weights_b, covariance, pair_0, near, far_0)
    got_0 = send(sent_0, swap_y)
    kept_1, sent_1, same_1, cross_1 = call(
        functools.partial(sweep_b, 1), (block,) * 2 + (shaped(1, 512, LEV),) * 2,
        [SMEM, VMEM] + [ANY] * 4 + [VMEM], (VMEM, VMEM, ANY, ANY),
        [field, field, dma(14), dma(2)], COST, "sweep_b1",
    )(coef_b, weights_b, covariance, pair_1, near, far_1, ends_b)
    kept_0, sent_0, same_1, cross_1, core = lax.optimization_barrier(
        (kept_0, sent_0, same_1, cross_1, core)
    )
    same_0 = send(kept_0, halo_same)
    cross_0 = send(sent_0, halo_cross)
    weights_a, ends_a, coef_a = call(
        prepare_a, (weight, ends, shaped(144)), [SMEM] * 3 + [VMEM] * 3, (VMEM, VMEM, SMEM),
        prep_scratch, 10**3, "prepare_a",
    )(table, winds, barriers, mix_a, across, core)
    sent_1, same_1, cross_1, got_0, weights_a = lax.optimization_barrier(
        (sent_1, same_1, cross_1, got_0, weights_a)
    )
    got_1 = send(sent_1, swap_y)
    same_1 = send(same_1, halo_same)
    cross_1 = send(cross_1, halo_flip)
    relay = send(got_0, relay_core)

    field = pltpu.VMEM((WINDOW, 512, LEV), F32)
    return call(
        sweep_a, shaped(512, 1024), [SMEM, VMEM, VMEM] + [ANY] * 9, VMEM, [field, field, dma(12)],
        4 * 10**3, "sweep_a",
    )(coef_a, weights_a, ends_a, kept_0, kept_1, got_0, got_1, same_0, same_1, cross_0, cross_1, relay)


def solution(mesh):
    placed = (P("row", "col"), P(), P(), P(), P("row", None, None), P("col", None, None))
    return jax.shard_map(
        functools.partial(per_device, mesh.shape["row"] // 4, mesh.shape["col"] // 2),
        mesh=mesh, in_specs=placed, out_specs=P("col", "row"), check_vma=False,
    )
```

```python
import functools
import itertools

import jax
import jax.numpy as jnp
from jax import lax
from jax.experimental import pallas as pl
from jax.experimental.pallas import tpu as pltpu
from jax.sharding import PartitionSpec as P

LAT = 128
LEV = 128
STEPS = 3
SPREAD = 0.15
WINDOW = 14
F32, BF16 = jnp.float32, jnp.bfloat16
COST = 4 * 10**9
AXES = ("row", "col")
ANY = pl.BlockSpec(memory_space=pl.ANY)
SMEM = pl.BlockSpec(memory_space=pltpu.SMEM)
VMEM = pl.BlockSpec(memory_space=pltpu.VMEM)


def pairs(move, x_size, z_size):
    number = lambda x, h, k, z, l: ((x * 2 + h) * 2 + k) * (2 * z_size) + z * 2 + l
    listed = []
    for x, h, k, z, l in itertools.product(range(x_size), range(2), range(2), range(z_size), range(2)):
        to = move(x, h, k, z, l)
        if to is not None and 0 <= to[0] < x_size and 0 <= to[3] < z_size:
            listed.append((number(x, h, k, z, l), number(*to)))
    return listed


def row_shift(x, h, k, by):
    at = (x * 2 + h) * 2 + k + by
    return at // 4, (at // 2) % 2, at % 2


def swap_y(x, h, k, z, l):
    return x, h, k, z, 1 - l


def near_z(x, h, k, z, l):
    return x, h, k, z + (1 if l else -1), l


def far_z(x, h, k, z, l):
    return x, h, k, z + (-1 if l else 1), l


def far_direct(x, h, k, z, l):
    return x, h, k, z + (1 if l else -1), 1 - l


def mats_across(size, x, h, k, z, l):
    tx, th, tk = row_shift(x, h, k, 1 if k else -1)
    return tx % size, th, tk, z, 1 - l


def mats_core(x, h, k, z, l):
    return x, h, 1 - k, z, l


def halo_same(x, h, k, z, l):
    return *row_shift(x, h, k, 1 if l else -1), z, l


def halo_cross(x, h, k, z, l):
    tx, th, tk = row_shift(x, h, k, 1 if l else -1)
    return None if (tx, th) == (x, h) else (tx, th, tk, z, 1 - l)


def relay_core(x, h, k, z, l):
    return (x, h, 1 - k, z, l) if k == l else None


def side():
    return lax.rem(lax.axis_index("col"), 2)


def turned(l, q, count):
    return jnp.where(l == 1, q, count - 1 - q)


def rows_of(l, chunk):
    return l * 768 if chunk == 0 else 256 + l * 256


def run_copies(copies, sems):
    started = []
    for i, (src, dst) in enumerate(copies):
        copy = pltpu.make_async_copy(src, dst, sems.at[i])
        copy.start()
        started.append(copy)
    for copy in started:
        copy.wait()


def lanes(start):
    return pl.ds(pl.multiple_of(start * LEV, LEV), LEV)


def rows(start, size):
    return pl.ds(pl.multiple_of(start, LEV), size)


def pack_mats(mix_a, mix_b, across, core, sems):
    k = lax.rem(lax.axis_index("row"), 2)
    run_copies(
        [
            (mix_b, across.at[pl.ds(0, 4)]),
            (mix_a.at[pl.ds(6 * k, 2)], across.at[pl.ds(4, 2)]),
            (mix_a.at[pl.ds(6 - 6 * k, 2)], core),
        ],
        sems,
    )


def pack_first(cov, first, sems):
    l = side()
    at = rows_of(1 - l, 0)
    copies = [(cov.at[rows(at, 256), lanes(l + i)], first.at[i]) for i in range(3)]
    run_copies(copies + [(cov.at[rows(at, 256), lanes(3 - 3 * l)], first.at[3])], sems)


def pack_near(cov, mix_b, near, sems):
    l = side()
    copies = []
    for c in range(2):
        for i in range(3):
            copies.append((cov.at[rows(rows_of(l, c), 256), lanes(l + i)], near.at[3 * c + i]))
    for m in range(2):
        copies.append((mix_b.at[2 * l + m], near.at[6, pl.ds(m * LEV, LEV)]))
    run_copies(copies, sems)


def pack_rest(cov, second, third, sems):
    l = side()
    at = rows_of(1 - l, 1)
    copies = []
    for i in range(3):
        copies.append((cov.at[rows(at, 256), lanes(l + i)], second.at[i]))
        copies.append((cov.at[rows(at, 256), lanes(l + i)], third.at[i]))
    run_copies(copies + [(cov.at[rows(at, 256), lanes(3 - 3 * l)], second.at[3])], sems)


def pack_edge(across, out, sems):
    l = side()
    run_copies([(across.at[pl.ds(2 - 2 * l, 2)], out)], sems)


def write_coefficients(l, base, tracer, table, winds, barriers, coef, flow):
    def interface(step, n):
        g = base + n - 3
        inside = (g >= 1) & (g <= LAT - 1)
        c = table[winds[tracer, step], jnp.clip(g, 0, LAT - 1)]
        blocked = barriers[0] == g
        for b in range(1, 4):
            blocked = blocked | (barriers[b] == g)
        c = c * jnp.where(blocked, 0.25, 1.0)
        flow[0, n] = jnp.where(inside, jnp.maximum(c, 0.0) + SPREAD, 0.0)
        flow[1, n] = jnp.where(inside, jnp.maximum(-c, 0.0) + SPREAD, 0.0)

    for step in range(STEPS):
        lax.fori_loop(0, WINDOW + 1, lambda n, _: interface(step, n), None)

        def place(p, _):
            n = turned(l, p, WINDOW)
            below, above = flow[0, n], flow[1, n + 1]
            coef[step * 48 + p] = jnp.where(l == 1, below, above)
            coef[step * 48 + 16 + p] = 1.0 - flow[1, n] - flow[0, n + 1]
            coef[step * 48 + 32 + p] = jnp.where(l == 1, above, below)

        lax.fori_loop(0, WINDOW, place, None)


def write_weight(weights, at, mixer):
    turned_mixer = mixer.T
    high = turned_mixer.astype(BF16)
    low = (turned_mixer - high.astype(F32)).astype(BF16)
    for half in range(2):
        weights[at, half * LEV : (half + 1) * LEV, :LEV] = high
        weights[at, half * LEV : (half + 1) * LEV, LEV:] = low


def prepare_b(table, winds, barriers, across, own, weights, coef, flow):
    l = side()
    base = lax.axis_index("col") // 2 * 8
    write_coefficients(l, base, 1, table, winds, barriers, coef, flow)
    for q in range(4):
        b = turned(l, q, 4)
        write_weight(weights, q, across[b])
        write_weight(weights, 4 + q, own[b])


def prepare_a(table, winds, barriers, own, across, core, weights, ends, coef, flow):
    l = side()
    k = lax.rem(lax.axis_index("row"), 2)
    base = lax.axis_index("row") * 8
    write_coefficients(l, base, 0, table, winds, barriers, coef, flow)
    for q in range(8):
        write_weight(weights, q, own[turned(l, q, 8)])
    for q in range(2):
        m = turned(l, q, 2)
        write_weight(ends, q, jnp.where(k == l, core[m], across[4 + m]))
        write_weight(ends, 2 + q, jnp.where(k == l, across[4 + m], core[m]))


def step_latitude(step, p, source, weights, ends, coef):
    weight = weights[p - 3] if 3 <= p <= 10 else ends[p - 1 if p < 3 else p - 9]
    y = (
        coef[step * 48 + p] * source[p - 1]
        + coef[step * 48 + 16 + p] * source[p]
        + coef[step * 48 + 32 + p] * source[p + 1]
    )
    high = y.astype(BF16)
    low = (y - high.astype(F32)).astype(BF16)
    both = jnp.dot(
        jnp.concatenate([high, low], axis=1), weight, preferred_element_type=F32
    )
    return both[:, :LEV] + both[:, LEV:]


def first_steps(window, other, weights, ends, coef):
    for p in range(1, WINDOW - 1):
        other[p] = step_latitude(0, p, window, weights, ends, coef)
    for p in range(2, WINDOW - 2):
        window[p] = step_latitude(1, p, other, weights, ends, coef)


def sweep_b(chunk, *refs):
    if chunk == 0:
        coef, weights, cov, pair, near, far, edge_far, kept, sent, ends, window, other, edge, sems = refs
    else:
        (coef, weights, cov, pair, near, far, ends, kept_before, sent_before,
         kept, sent, same, cross, window, other, sems, late) = refs
    l = side()
    copies = []
    for q in range(3):
        t = turned(l, q, 3)
        copies.append((near.at[3 * chunk + t], window.at[q]))
        copies.append((pair.at[t], window.at[3 + q]))
        copies.append((far.at[t], window.at[11 + q]))
    copies.append((pair.at[3], window.at[6]))
    for q in range(4):
        copies.append((cov.at[rows(rows_of(l, chunk), 256), lanes(turned(l, q, 4))], window.at[7 + q]))
    if chunk == 0:
        for m in range(2):
            copies.append((near.at[6, pl.ds(m * LEV, LEV)], edge.at[m]))
            copies.append((edge_far.at[m], edge.at[2 + m]))
    run_copies(copies, sems)
    if chunk == 0:
        for place in range(2):
            for q in range(2):
                m = turned(l, q, 2)
                write_weight(ends, 2 * place + q, edge[2 * place + m])
    first_steps(window, other, weights, ends, coef)

    def finish(p, target, q):
        z = step_latitude(2, p, window, weights, ends, coef)
        b = turned(l, q, 4)
        for i in range(2):
            u = turned(l, i, 2)
            target[u, rows(b * LEV, LEV), :] = z[i * LEV : (i + 1) * LEV].T

    for q in range(4):
        finish(3 + q, sent, q)
    for q in range(4):
        finish(7 + q, kept, q)
    if chunk == 1:
        run_copies(
            [
                (kept_before, same.at[pl.ds(1, 2)]),
                (sent_before, cross.at[pl.ds(1, 2)]),
                (kept.at[1], same.at[0]),
                (sent.at[1], cross.at[0]),
            ],
            late,
        )


def sweep_a(coef, weights, ends, kept_0, kept_1, got_0, got_1, same, cross, relay_0, relay_1, out,
            window, other, sems):
    l = side()
    k = lax.rem(lax.axis_index("row"), 2)
    copies = [(same.at[q], window.at[q]) for q in range(3)]
    for u in range(2):
        copies.append((kept_1.at[u], window.at[7 + u]))
        copies.append((kept_0.at[u], window.at[9 + u]))
        copies.append((got_0.at[u], window.at[4 - u]))
        copies.append((got_1.at[u], window.at[6 - u]))
    across = [(cross.at[q], window.at[13 - q]) for q in range(3)]
    inside = [(relay_1.at[0], window.at[13])] + [(relay_0.at[u], window.at[12 - u]) for u in range(2)]

    @pl.when(k == l)
    def _():
        run_copies(across, sems)

    @pl.when(k != l)
    def _():
        run_copies(inside, sems)

    run_copies(copies, sems)
    first_steps(window, other, weights, ends, coef)

    for p in range(3, WINDOW - 3):
        out[:, lanes(turned(l, p - 3, 8))] = step_latitude(2, p, window, weights, ends, coef)


def pack(kernel, outs, operands, copies, name):
    return pl.pallas_call(
        kernel,
        out_shape=outs,
        in_specs=[ANY] * operands,
        out_specs=ANY if isinstance(outs, jax.ShapeDtypeStruct) else (ANY,) * len(outs),
        scratch_shapes=[pltpu.SemaphoreType.DMA((copies,))],
        compiler_params=pltpu.CompilerParams(vmem_limit_bytes=40 * 1024 * 1024),
        cost_estimate=pl.CostEstimate(flops=0, bytes_accessed=2**10, transcendentals=0),
        name=name,
    )


def call(kernel, outs, in_specs, out_specs, scratch, flops, name):
    return pl.pallas_call(
        kernel,
        out_shape=outs,
        in_specs=in_specs,
        out_specs=out_specs,
        scratch_shapes=scratch,
        compiler_params=pltpu.CompilerParams(vmem_limit_bytes=40 * 1024 * 1024),
        cost_estimate=pl.CostEstimate(flops=flops, bytes_accessed=2**10, transcendentals=0),
        name=name,
    )


def shaped(*dims, dtype=F32):
    return jax.ShapeDtypeStruct(dims, dtype)


def per_device(x_size, z_size, covariance, table, winds, barriers, mix_a, mix_b):
    send = lambda value, move: lax.ppermute(value, AXES, pairs(move, x_size, z_size))
    dma = lambda n: pltpu.SemaphoreType.DMA((n,))

    piece = lambda n: shaped(n, 256, LEV)
    out_0 = pack(pack_first, piece(4), 1, 4, "pack_first")(covariance)
    pair_0 = send(out_0, swap_y)
    mix_a, mix_b, out_0 = lax.optimization_barrier((mix_a, mix_b, out_0))
    out_across, out_core = pack(
        pack_mats, (shaped(6, LEV, LEV), shaped(2, LEV, LEV)), 2, 3, "pack_mats"
    )(mix_a, mix_b)
    across = send(out_across, functools.partial(mats_across, x_size))
    core = send(out_core, mats_core)
    covariance, out_across = lax.optimization_barrier((covariance, out_across))
    out_near = pack(pack_near, piece(7), 2, 8, "pack_near")(covariance, mix_b)
    near = send(out_near, near_z)
    out_1, out_far_1 = pack(pack_rest, (piece(4), piece(3)), 1, 7, "pack_rest")(covariance)
    out_1, core = lax.optimization_barrier((out_1, core))
    pair_1 = send(out_1, swap_y)
    pair_0, across = lax.optimization_barrier((pair_0, across))
    far_0 = send(pair_0[:3], far_z)
    edge_far = send(pack(pack_edge, shaped(2, LEV, LEV), 1, 1, "pack_edge")(across), far_z)
    out_far_1, pair_1 = lax.optimization_barrier((out_far_1, pair_1))
    far_1 = send(out_far_1, far_direct)

    weight = shaped(8, 256, 256, dtype=BF16)
    ends = shaped(4, 256, 256, dtype=BF16)
    prep_scratch = [pltpu.SMEM((2, 16), F32)]
    weights_b, coef_b = call(
        prepare_b, (weight, shaped(144)), [SMEM] * 3 + [VMEM] * 2, (VMEM, SMEM), prep_scratch, 10**3,
        "prepare_b",
    )(table, winds, barriers, across, mix_b)
    weights_a, ends_a, coef_a = call(
        prepare_a, (weight, ends, shaped(144)), [SMEM] * 3 + [VMEM] * 3, (VMEM, VMEM, SMEM),
        prep_scratch, 10**3, "prepare_a",
    )(table, winds, barriers, mix_a, across, core)
    weights_b, weights_a, far_0, pair_1 = lax.optimization_barrier((weights_b, weights_a, far_0, pair_1))
    block = shaped(2, 512, LEV)
    field = pltpu.VMEM((WINDOW, 256, LEV), F32)
    kept_0, sent_0, ends_b = call(
        functools.partial(sweep_b, 0), (block, block, ends), [SMEM, VMEM] + [ANY] * 5, (VMEM,) * 3,
        [field, field, pltpu.VMEM((4, LEV, LEV), F32), dma(18)], COST, "sweep_b0",
    )(coef_b, weights_b, covariance, pair_0, near, far_0, edge_far)
    got_0 = send(sent_0, swap_y)
    kept_1, sent_1, out_same, out_cross = call(
        functools.partial(sweep_b, 1), (block,) * 2 + (shaped(3, 512, LEV),) * 2,
        [SMEM, VMEM] + [ANY] * 4 + [VMEM] + [ANY] * 2, (VMEM, VMEM, ANY, ANY),
        [field, field, dma(14), dma(4)], COST, "sweep_b1",
    )(coef_b, weights_b, covariance, pair_1, near, far_1, ends_b, kept_0, sent_0)
    got_1 = send(sent_1, swap_y)
    out_same, got_0 = lax.optimization_barrier((out_same, got_0))
    same = send(out_same, halo_same)
    cross = send(out_cross, halo_cross)
    relay_0 = send(got_0, relay_core)
    relay_1 = send(got_1[1:], relay_core)

    field = pltpu.VMEM((WINDOW, 512, LEV), F32)
    return call(
        sweep_a, shaped(512, 1024), [SMEM, VMEM, VMEM] + [ANY] * 8, VMEM, [field, field, dma(11)],
        4 * 10**3, "sweep_a",
    )(coef_a, weights_a, ends_a, kept_0, kept_1, got_0, got_1, same, cross, relay_0, relay_1)


def solution(mesh):
    placed = (P("row", "col"), P(), P(), P(), P("row", None, None), P("col", None, None))
    return jax.shard_map(
        functools.partial(per_device, mesh.shape["row"] // 4, mesh.shape["col"] // 2),
        mesh=mesh, in_specs=placed, out_specs=P("col", "row"), check_vma=False,
    )
```

```python
import functools
import itertools

import jax
import jax.numpy as jnp
from jax import lax
from jax.experimental import pallas as pl
from jax.experimental.pallas import tpu as pltpu
from jax.sharding import PartitionSpec as P

LAT = 128
LEV = 128
STEPS = 3
SPREAD = 0.15
WINDOW = 14
F32, BF16 = jnp.float32, jnp.bfloat16
COST = 4 * 10**9
AXES = ("row", "col")
ANY = pl.BlockSpec(memory_space=pl.ANY)
SMEM = pl.BlockSpec(memory_space=pltpu.SMEM)
VMEM = pl.BlockSpec(memory_space=pltpu.VMEM)


def pairs(move, x_size, z_size):
    number = lambda x, h, k, z, l: ((x * 2 + h) * 2 + k) * (2 * z_size) + z * 2 + l
    listed = []
    for x, h, k, z, l in itertools.product(range(x_size), range(2), range(2), range(z_size), range(2)):
        to = move(x, h, k, z, l)
        if to is not None and 0 <= to[0] < x_size and 0 <= to[3] < z_size:
            listed.append((number(x, h, k, z, l), number(*to)))
    return listed


def row_shift(x, h, k, by):
    at = (x * 2 + h) * 2 + k + by
    return at // 4, (at // 2) % 2, at % 2


def swap_y(x, h, k, z, l):
    return x, h, k, z, 1 - l


def near_z(x, h, k, z, l):
    return x, h, k, z + (1 if l else -1), l


def far_z(x, h, k, z, l):
    return x, h, k, z + (-1 if l else 1), l


def far_direct(x, h, k, z, l):
    return x, h, k, z + (1 if l else -1), 1 - l


def mats_across(size, x, h, k, z, l):
    tx, th, tk = row_shift(x, h, k, 1 if k else -1)
    return tx % size, th, tk, z, 1 - l


def mats_core(x, h, k, z, l):
    return x, h, 1 - k, z, l


def halo_same(x, h, k, z, l):
    return *row_shift(x, h, k, 1 if l else -1), z, l


def halo_cross(x, h, k, z, l):
    tx, th, tk = row_shift(x, h, k, 1 if l else -1)
    return None if (tx, th) == (x, h) else (tx, th, tk, z, 1 - l)


def relay_core(x, h, k, z, l):
    return (x, h, 1 - k, z, l) if k == l else None


def side():
    return lax.rem(lax.axis_index("col"), 2)


def turned(l, q, count):
    return jnp.where(l == 1, q, count - 1 - q)


def rows_of(l, chunk):
    return l * 768 if chunk == 0 else 256 + l * 256


def run_copies(copies, sems):
    started = []
    for i, (src, dst) in enumerate(copies):
        copy = pltpu.make_async_copy(src, dst, sems.at[i])
        copy.start()
        started.append(copy)
    for copy in started:
        copy.wait()


def lanes(start):
    return pl.ds(pl.multiple_of(start * LEV, LEV), LEV)


def rows(start, size):
    return pl.ds(pl.multiple_of(start, LEV), size)


def pack_first(cov, first, sems):
    l = side()
    at = rows_of(1 - l, 0)
    copies = [(cov.at[rows(at, 256), lanes(l + i)], first.at[i]) for i in range(3)]
    run_copies(copies + [(cov.at[rows(at, 256), lanes(3 - 3 * l)], first.at[3])], sems)


def pack_second(cov, mix_a, mix_b, across, near, core, sems):
    l = side()
    k = lax.rem(lax.axis_index("row"), 2)
    copies = [
        (mix_b, across.at[pl.ds(0, 4)]),
        (mix_a.at[pl.ds(6 * k, 2)], across.at[pl.ds(4, 2)]),
        (mix_a.at[pl.ds(6 - 6 * k, 2)], core),
    ]
    for c in range(2):
        for i in range(3):
            copies.append((cov.at[rows(rows_of(l, c), 256), lanes(l + i)], near.at[3 * c + i]))
    for m in range(2):
        copies.append((mix_b.at[2 * l + m], near.at[6, pl.ds(m * LEV, LEV)]))
    run_copies(copies, sems)


def pack_rest(cov, second, third, sems):
    l = side()
    at = rows_of(1 - l, 1)
    copies = []
    for i in range(3):
        copies.append((cov.at[rows(at, 256), lanes(l + i)], second.at[i]))
        copies.append((cov.at[rows(at, 256), lanes(l + i)], third.at[i]))
    run_copies(copies + [(cov.at[rows(at, 256), lanes(3 - 3 * l)], second.at[3])], sems)


def pack_far(pair, across, out, sems):
    l = side()
    copies = [(pair.at[pl.ds(0, 3)], out.at[pl.ds(0, 3)])]
    for m in range(2):
        copies.append((across.at[2 - 2 * l + m], out.at[3, pl.ds(m * LEV, LEV)]))
    run_copies(copies, sems)


def write_coefficients(l, base, tracer, table, winds, barriers, coef, flow):
    def interface(step, n):
        g = base + n - 3
        inside = (g >= 1) & (g <= LAT - 1)
        c = table[winds[tracer, step], jnp.clip(g, 0, LAT - 1)]
        blocked = barriers[0] == g
        for b in range(1, 4):
            blocked = blocked | (barriers[b] == g)
        c = c * jnp.where(blocked, 0.25, 1.0)
        flow[0, n] = jnp.where(inside, jnp.maximum(c, 0.0) + SPREAD, 0.0)
        flow[1, n] = jnp.where(inside, jnp.maximum(-c, 0.0) + SPREAD, 0.0)

    for step in range(STEPS):
        lax.fori_loop(0, WINDOW + 1, lambda n, _: interface(step, n), None)

        def place(p, _):
            n = turned(l, p, WINDOW)
            below, above = flow[0, n], flow[1, n + 1]
            coef[step * 48 + p] = jnp.where(l == 1, below, above)
            coef[step * 48 + 16 + p] = 1.0 - flow[1, n] - flow[0, n + 1]
            coef[step * 48 + 32 + p] = jnp.where(l == 1, above, below)

        lax.fori_loop(0, WINDOW, place, None)


def write_weight(weights, at, mixer):
    turned_mixer = mixer.T
    high = turned_mixer.astype(BF16)
    low = (turned_mixer - high.astype(F32)).astype(BF16)
    for half in range(2):
        weights[at, half * LEV : (half + 1) * LEV, :LEV] = high
        weights[at, half * LEV : (half + 1) * LEV, LEV:] = low


def prepare_b(table, winds, barriers, across, own, weights, coef, flow):
    l = side()
    base = lax.axis_index("col") // 2 * 8
    write_coefficients(l, base, 1, table, winds, barriers, coef, flow)
    for q in range(4):
        b = turned(l, q, 4)
        write_weight(weights, q, across[b])
        write_weight(weights, 4 + q, own[b])


def prepare_a(table, winds, barriers, own, across, core, weights, ends, coef, flow):
    l = side()
    k = lax.rem(lax.axis_index("row"), 2)
    base = lax.axis_index("row") * 8
    write_coefficients(l, base, 0, table, winds, barriers, coef, flow)
    for q in range(8):
        write_weight(weights, q, own[turned(l, q, 8)])
    for q in range(2):
        m = turned(l, q, 2)
        write_weight(ends, q, jnp.where(k == l, core[m], across[4 + m]))
        write_weight(ends, 2 + q, jnp.where(k == l, across[4 + m], core[m]))


def step_latitude(step, p, source, weights, ends, coef):
    weight = weights[p - 3] if 3 <= p <= 10 else ends[p - 1 if p < 3 else p - 9]
    y = (
        coef[step * 48 + p] * source[p - 1]
        + coef[step * 48 + 16 + p] * source[p]
        + coef[step * 48 + 32 + p] * source[p + 1]
    )
    high = y.astype(BF16)
    low = (y - high.astype(F32)).astype(BF16)
    both = jnp.dot(
        jnp.concatenate([high, low], axis=1), weight, preferred_element_type=F32
    )
    return both[:, :LEV] + both[:, LEV:]


def first_steps(window, other, weights, ends, coef):
    for p in range(1, WINDOW - 1):
        other[p] = step_latitude(0, p, window, weights, ends, coef)
    for p in range(2, WINDOW - 2):
        window[p] = step_latitude(1, p, other, weights, ends, coef)


def sweep_b(chunk, *refs):
    if chunk == 0:
        coef, weights, cov, pair, near, far, kept, sent, ends, window, other, edge, sems = refs
    else:
        (coef, weights, cov, pair, near, far, ends, kept_before, sent_before,
         kept, sent, same, cross, window, other, sems, late) = refs
    l = side()
    copies = []
    for q in range(3):
        t = turned(l, q, 3)
        copies.append((near.at[3 * chunk + t], window.at[q]))
        copies.append((pair.at[t], window.at[3 + q]))
        copies.append((far.at[t], window.at[11 + q]))
    copies.append((pair.at[3], window.at[6]))
    for q in range(4):
        copies.append((cov.at[rows(rows_of(l, chunk), 256), lanes(turned(l, q, 4))], window.at[7 + q]))
    if chunk == 0:
        for m in range(2):
            copies.append((near.at[6, pl.ds(m * LEV, LEV)], edge.at[m]))
            copies.append((far.at[3, pl.ds(m * LEV, LEV)], edge.at[2 + m]))
    run_copies(copies, sems)
    if chunk == 0:
        for place in range(2):
            for q in range(2):
                m = turned(l, q, 2)
                write_weight(ends, 2 * place + q, edge[2 * place + m])
    first_steps(window, other, weights, ends, coef)

    def finish(p, target, q):
        z = step_latitude(2, p, window, weights, ends, coef)
        b = turned(l, q, 4)
        for i in range(2):
            u = turned(l, i, 2)
            target[u, rows(b * LEV, LEV), :] = z[i * LEV : (i + 1) * LEV].T

    for q in range(4):
        finish(3 + q, sent, q)
    for q in range(4):
        finish(7 + q, kept, q)
    if chunk == 1:
        run_copies(
            [
                (kept_before, same.at[pl.ds(1, 2)]),
                (sent_before, cross.at[pl.ds(1, 2)]),
                (kept.at[1], same.at[0]),
                (sent.at[1], cross.at[0]),
            ],
            late,
        )


def sweep_a(coef, weights, ends, kept_0, kept_1, got_0, got_1, same, cross, relay_0, relay_1, out,
            window, other, sems):
    l = side()
    k = lax.rem(lax.axis_index("row"), 2)
    copies = [(same.at[q], window.at[q]) for q in range(3)]
    for u in range(2):
        copies.append((kept_1.at[u], window.at[7 + u]))
        copies.append((kept_0.at[u], window.at[9 + u]))
        copies.append((got_0.at[u], window.at[4 - u]))
        copies.append((got_1.at[u], window.at[6 - u]))
    across = [(cross.at[q], window.at[13 - q]) for q in range(3)]
    inside = [(relay_1.at[0], window.at[13])] + [(relay_0.at[u], window.at[12 - u]) for u in range(2)]

    @pl.when(k == l)
    def _():
        run_copies(across, sems)

    @pl.when(k != l)
    def _():
        run_copies(inside, sems)

    run_copies(copies, sems)
    first_steps(window, other, weights, ends, coef)

    for p in range(3, WINDOW - 3):
        out[:, lanes(turned(l, p - 3, 8))] = step_latitude(2, p, window, weights, ends, coef)


def pack(kernel, outs, operands, copies, name):
    return pl.pallas_call(
        kernel,
        out_shape=outs,
        in_specs=[ANY] * operands,
        out_specs=ANY if isinstance(outs, jax.ShapeDtypeStruct) else (ANY,) * len(outs),
        scratch_shapes=[pltpu.SemaphoreType.DMA((copies,))],
        compiler_params=pltpu.CompilerParams(vmem_limit_bytes=40 * 1024 * 1024),
        cost_estimate=pl.CostEstimate(flops=0, bytes_accessed=2**10, transcendentals=0),
        name=name,
    )


def call(kernel, outs, in_specs, out_specs, scratch, flops, name):
    return pl.pallas_call(
        kernel,
        out_shape=outs,
        in_specs=in_specs,
        out_specs=out_specs,
        scratch_shapes=scratch,
        compiler_params=pltpu.CompilerParams(vmem_limit_bytes=40 * 1024 * 1024),
        cost_estimate=pl.CostEstimate(flops=flops, bytes_accessed=2**10, transcendentals=0),
        name=name,
    )


def shaped(*dims, dtype=F32):
    return jax.ShapeDtypeStruct(dims, dtype)


def per_device(x_size, z_size, covariance, table, winds, barriers, mix_a, mix_b):
    send = lambda value, move: lax.ppermute(value, AXES, pairs(move, x_size, z_size))
    dma = lambda n: pltpu.SemaphoreType.DMA((n,))

    piece = lambda n: shaped(n, 256, LEV)
    out_0 = pack(pack_first, piece(4), 1, 4, "pack_first")(covariance)
    pair_0 = send(out_0, swap_y)
    covariance, mix_a, mix_b, out_0 = lax.optimization_barrier((covariance, mix_a, mix_b, out_0))
    out_across, out_near, out_core = pack(
        pack_second, (shaped(6, LEV, LEV), piece(7), shaped(2, LEV, LEV)), 3, 11, "pack_second"
    )(covariance, mix_a, mix_b)
    across = send(out_across, functools.partial(mats_across, x_size))
    near = send(out_near, near_z)
    covariance, out_across = lax.optimization_barrier((covariance, out_across))
    out_1, out_far_1 = pack(pack_rest, (piece(4), piece(3)), 1, 7, "pack_rest")(covariance)
    pair_1 = send(out_1, swap_y)
    out_far_0 = pack(pack_far, piece(4), 2, 3, "pack_far")(pair_0, across)
    far_0 = send(out_far_0, far_z)
    out_far_1, pair_1 = lax.optimization_barrier((out_far_1, pair_1))
    far_1 = send(out_far_1, far_direct)

    weight = shaped(8, 256, 256, dtype=BF16)
    ends = shaped(4, 256, 256, dtype=BF16)
    prep_scratch = [pltpu.SMEM((2, 16), F32)]
    weights_b, coef_b = call(
        prepare_b, (weight, shaped(144)), [SMEM] * 3 + [VMEM] * 2, (VMEM, SMEM), prep_scratch, 10**3,
        "prepare_b",
    )(table, winds, barriers, across, mix_b)
    weights_b, far_0, pair_1 = lax.optimization_barrier((weights_b, far_0, pair_1))
    block = shaped(2, 512, LEV)
    field = pltpu.VMEM((WINDOW, 256, LEV), F32)
    kept_0, sent_0, ends_b = call(
        functools.partial(sweep_b, 0), (block, block, ends), [SMEM, VMEM] + [ANY] * 4, (VMEM,) * 3,
        [field, field, pltpu.VMEM((4, LEV, LEV), F32), dma(18)], COST, "sweep_b0",
    )(coef_b, weights_b, covariance, pair_0, near, far_0)
    got_0 = send(sent_0, swap_y)
    kept_1, sent_1, out_same, out_cross = call(
        functools.partial(sweep_b, 1), (block, block, shaped(3, 512, LEV), shaped(3, 512, LEV)),
        [SMEM, VMEM] + [ANY] * 4 + [VMEM, ANY, ANY], (VMEM, VMEM, ANY, ANY),
        [field, field, dma(14), dma(4)], COST, "sweep_b1",
    )(coef_b, weights_b, covariance, pair_1, near, far_1, ends_b, kept_0, sent_0)
    got_1 = send(sent_1, swap_y)
    cross = send(out_cross, halo_cross)
    out_same, out_core, got_0 = lax.optimization_barrier((out_same, out_core, got_0))
    same = send(out_same, halo_same)
    core = send(out_core, mats_core)
    weights_a, ends_a, coef_a = call(
        prepare_a, (weight, ends, shaped(144)), [SMEM] * 3 + [VMEM] * 3, (VMEM, VMEM, SMEM),
        prep_scratch, 10**3, "prepare_a",
    )(table, winds, barriers, mix_a, across, core)
    got_0, weights_a = lax.optimization_barrier((got_0, weights_a))
    relay_0 = send(got_0, relay_core)
    relay_1 = send(got_1[1:], relay_core)

    field = pltpu.VMEM((WINDOW, 512, LEV), F32)
    return call(
        sweep_a, shaped(512, 1024), [SMEM, VMEM, VMEM] + [ANY] * 8, VMEM, [field, field, dma(11)],
        4 * 10**3, "sweep_a",
    )(coef_a, weights_a, ends_a, kept_0, kept_1, got_0, got_1, same, cross, relay_0, relay_1)


def solution(mesh):
    placed = (P("row", "col"), P(), P(), P(), P("row", None, None), P("col", None, None))
    return jax.shard_map(
        functools.partial(per_device, mesh.shape["row"] // 4, mesh.shape["col"] // 2),
        mesh=mesh, in_specs=placed, out_specs=P("col", "row"), check_vma=False,
    )
```

```python
import functools
import itertools

import jax
import jax.numpy as jnp
from jax import lax
from jax.experimental import pallas as pl
from jax.experimental.pallas import tpu as pltpu
from jax.sharding import PartitionSpec as P

LAT = 128
LEV = 128
STEPS = 3
SPREAD = 0.15
WINDOW = 14
F32, BF16 = jnp.float32, jnp.bfloat16
COST = 4 * 10**9
AXES = ("row", "col")
ANY = pl.BlockSpec(memory_space=pl.ANY)
SMEM = pl.BlockSpec(memory_space=pltpu.SMEM)
VMEM = pl.BlockSpec(memory_space=pltpu.VMEM)


def pairs(move, x_size, z_size):
    number = lambda x, h, k, z, l: ((x * 2 + h) * 2 + k) * (2 * z_size) + z * 2 + l
    listed = []
    for x, h, k, z, l in itertools.product(range(x_size), range(2), range(2), range(z_size), range(2)):
        to = move(x, h, k, z, l)
        if to is not None and 0 <= to[0] < x_size and 0 <= to[3] < z_size:
            listed.append((number(x, h, k, z, l), number(*to)))
    return listed


def row_shift(x, h, k, by):
    at = (x * 2 + h) * 2 + k + by
    return at // 4, (at // 2) % 2, at % 2


def swap_y(x, h, k, z, l):
    return x, h, k, z, 1 - l


def near_z(x, h, k, z, l):
    return x, h, k, z + (1 if l else -1), l


def far_z(x, h, k, z, l):
    return x, h, k, z + (-1 if l else 1), l


def far_direct(x, h, k, z, l):
    return x, h, k, z + (1 if l else -1), 1 - l


def mats_across(size, x, h, k, z, l):
    tx, th, tk = row_shift(x, h, k, 1 if k else -1)
    return tx % size, th, tk, z, 1 - l


def mats_core(x, h, k, z, l):
    return x, h, 1 - k, z, l


def halo_same(x, h, k, z, l):
    return *row_shift(x, h, k, 1 if l else -1), z, l


def halo_cross(x, h, k, z, l):
    tx, th, tk = row_shift(x, h, k, 1 if l else -1)
    return None if (tx, th) == (x, h) else (tx, th, tk, z, 1 - l)


def relay_core(x, h, k, z, l):
    return (x, h, 1 - k, z, l) if k == l else None


def side():
    return lax.rem(lax.axis_index("col"), 2)


def turned(l, q, count):
    return jnp.where(l == 1, q, count - 1 - q)


def rows_of(l, chunk):
    return l * 768 if chunk == 0 else 256 + l * 256


def run_copies(copies, sems):
    started = []
    for i, (src, dst) in enumerate(copies):
        copy = pltpu.make_async_copy(src, dst, sems.at[i])
        copy.start()
        started.append(copy)
    for copy in started:
        copy.wait()


def lanes(start):
    return pl.ds(pl.multiple_of(start * LEV, LEV), LEV)


def rows(start, size):
    return pl.ds(pl.multiple_of(start, LEV), size)


def pack_first(cov, first, sems):
    run_copies([(cov.at[rows(rows_of(1 - side(), 0), 256)], first)], sems)


def pack_second(cov, mix_a, mix_b, across, near, core, sems):
    l = side()
    k = lax.rem(lax.axis_index("row"), 2)
    copies = [
        (mix_b, across.at[pl.ds(0, 4)]),
        (mix_a.at[pl.ds(6 * k, 2)], across.at[pl.ds(4, 2)]),
        (mix_a.at[pl.ds(6 - 6 * k, 2)], core),
    ]
    for c in range(2):
        for i in range(3):
            copies.append((cov.at[rows(rows_of(l, c), 256), lanes(l + i)], near.at[3 * c + i]))
    for m in range(2):
        copies.append((mix_b.at[2 * l + m], near.at[6, pl.ds(m * LEV, LEV)]))
    run_copies(copies, sems)


def pack_rest(cov, second, third, sems):
    l = side()
    at = rows_of(1 - l, 1)
    copies = [(cov.at[rows(at, 256)], second)]
    run_copies(copies + [(cov.at[rows(at, 256), lanes(l + i)], third.at[i]) for i in range(3)], sems)


def pack_far(pair, across, out, sems):
    l = side()
    copies = [(pair.at[:, lanes(1 - l + i)], out.at[i]) for i in range(3)]
    for m in range(2):
        copies.append((across.at[2 - 2 * l + m], out.at[3, pl.ds(m * LEV, LEV)]))
    run_copies(copies, sems)


def write_coefficients(l, base, tracer, table, winds, barriers, coef, flow):
    def interface(step, n):
        g = base + n - 3
        inside = (g >= 1) & (g <= LAT - 1)
        c = table[winds[tracer, step], jnp.clip(g, 0, LAT - 1)]
        blocked = barriers[0] == g
        for b in range(1, 4):
            blocked = blocked | (barriers[b] == g)
        c = c * jnp.where(blocked, 0.25, 1.0)
        flow[0, n] = jnp.where(inside, jnp.maximum(c, 0.0) + SPREAD, 0.0)
        flow[1, n] = jnp.where(inside, jnp.maximum(-c, 0.0) + SPREAD, 0.0)

    for step in range(STEPS):
        lax.fori_loop(0, WINDOW + 1, lambda n, _: interface(step, n), None)

        def place(p, _):
            n = turned(l, p, WINDOW)
            below, above = flow[0, n], flow[1, n + 1]
            coef[step * 48 + p] = jnp.where(l == 1, below, above)
            coef[step * 48 + 16 + p] = 1.0 - flow[1, n] - flow[0, n + 1]
            coef[step * 48 + 32 + p] = jnp.where(l == 1, above, below)

        lax.fori_loop(0, WINDOW, place, None)


def write_weight(weights, at, mixer):
    turned_mixer = mixer.T
    high = turned_mixer.astype(BF16)
    low = (turned_mixer - high.astype(F32)).astype(BF16)
    for half in range(2):
        weights[at, half * LEV : (half + 1) * LEV, :LEV] = high
        weights[at, half * LEV : (half + 1) * LEV, LEV:] = low


def prepare_b(table, winds, barriers, across, own, weights, coef, flow):
    l = side()
    base = lax.axis_index("col") // 2 * 8
    write_coefficients(l, base, 1, table, winds, barriers, coef, flow)
    for q in range(4):
        b = turned(l, q, 4)
        write_weight(weights, q, across[b])
        write_weight(weights, 4 + q, own[b])


def prepare_a(table, winds, barriers, own, across, core, weights, ends, coef, flow):
    l = side()
    k = lax.rem(lax.axis_index("row"), 2)
    base = lax.axis_index("row") * 8
    write_coefficients(l, base, 0, table, winds, barriers, coef, flow)
    for q in range(8):
        write_weight(weights, q, own[turned(l, q, 8)])
    for q in range(2):
        m = turned(l, q, 2)
        write_weight(ends, q, jnp.where(k == l, core[m], across[4 + m]))
        write_weight(ends, 2 + q, jnp.where(k == l, across[4 + m], core[m]))


def step_latitude(step, p, source, weights, ends, coef):
    weight = weights[p - 3] if 3 <= p <= 10 else ends[p - 1 if p < 3 else p - 9]
    y = (
        coef[step * 48 + p] * source(p - 1)
        + coef[step * 48 + 16 + p] * source(p)
        + coef[step * 48 + 32 + p] * source(p + 1)
    )
    high = y.astype(BF16)
    low = (y - high.astype(F32)).astype(BF16)
    both = jnp.dot(
        jnp.concatenate([high, low], axis=1), weight, preferred_element_type=F32
    )
    return both[:, :LEV] + both[:, LEV:]


def first_steps(source, window, other, weights, ends, coef):
    for p in range(1, WINDOW - 1):
        other[p] = step_latitude(0, p, source, weights, ends, coef)
    for p in range(2, WINDOW - 2):
        window[p] = step_latitude(1, p, lambda at: other[at], weights, ends, coef)


def sweep_b(chunk, *refs):
    if chunk == 0:
        coef, weights, cov, pair, near, far, kept, sent, ends, window, other = refs
    else:
        (coef, weights, cov, pair, near, far, ends, kept_before, sent_before,
         kept, sent, same, cross, window, other, late) = refs
    l = side()

    def source(p):
        if p < 3:
            return near[3 * chunk + turned(l, p, 3)]
        if p < 7:
            return pair[:, lanes(turned(l, p - 3, 4))]
        if p < 11:
            return cov[rows(rows_of(l, chunk), 256), lanes(turned(l, p - 7, 4))]
        return far[turned(l, p - 11, 3)]

    if chunk == 0:
        for q in range(2):
            at = rows(turned(l, q, 2) * LEV, LEV)
            write_weight(ends, q, near[6, at, :])
            write_weight(ends, 2 + q, far[3, at, :])
    first_steps(source, window, other, weights, ends, coef)

    def finish(p, target, q):
        z = step_latitude(2, p, lambda at: window[at], weights, ends, coef)
        b = turned(l, q, 4)
        for i in range(2):
            u = turned(l, i, 2)
            target[u, rows(b * LEV, LEV), :] = z[i * LEV : (i + 1) * LEV].T

    for q in range(4):
        finish(3 + q, sent, q)
    for q in range(4):
        finish(7 + q, kept, q)
    if chunk == 1:
        run_copies(
            [
                (kept_before, same.at[pl.ds(1, 2)]),
                (sent_before, cross.at[pl.ds(1, 2)]),
                (kept.at[1], same.at[0]),
                (sent.at[1], cross.at[0]),
            ],
            late,
        )


def sweep_a(coef, weights, ends, kept_0, kept_1, got_0, got_1, same, cross, relay_0, relay_1, out,
            window, other, sems):
    l = side()
    k = lax.rem(lax.axis_index("row"), 2)

    @pl.when(k == l)
    def _():
        run_copies([(cross.at[q], window.at[13 - q]) for q in range(3)], sems)

    @pl.when(k != l)
    def _():
        copies = [(relay_0.at[u], window.at[12 - u]) for u in range(2)]
        run_copies(copies + [(relay_1.at[0], window.at[13])], sems)

    def source(p):
        if p < 3:
            return same[p]
        if p < 7:
            return (got_0, got_1)[p > 4][p % 2 if p > 4 else 4 - p]
        if p < 11:
            return (kept_1, kept_0)[p > 8][1 - p % 2]
        return window[p]

    first_steps(source, window, other, weights, ends, coef)
    for p in range(3, WINDOW - 3):
        out[:, lanes(turned(l, p - 3, 8))] = step_latitude(
            2, p, lambda at: window[at], weights, ends, coef
        )


def pack(kernel, outs, operands, copies, name):
    return pl.pallas_call(
        kernel,
        out_shape=outs,
        in_specs=[ANY] * operands,
        out_specs=ANY if isinstance(outs, jax.ShapeDtypeStruct) else (ANY,) * len(outs),
        scratch_shapes=[pltpu.SemaphoreType.DMA((copies,))],
        compiler_params=pltpu.CompilerParams(vmem_limit_bytes=40 * 1024 * 1024),
        cost_estimate=pl.CostEstimate(flops=0, bytes_accessed=2**10, transcendentals=0),
        name=name,
    )


def call(kernel, outs, in_specs, out_specs, scratch, flops, name):
    return pl.pallas_call(
        kernel,
        out_shape=outs,
        in_specs=in_specs,
        out_specs=out_specs,
        scratch_shapes=scratch,
        compiler_params=pltpu.CompilerParams(vmem_limit_bytes=40 * 1024 * 1024),
        cost_estimate=pl.CostEstimate(flops=flops, bytes_accessed=2**10, transcendentals=0),
        name=name,
    )


def shaped(*dims, dtype=F32):
    return jax.ShapeDtypeStruct(dims, dtype)


def per_device(x_size, z_size, covariance, table, winds, barriers, mix_a, mix_b):
    send = lambda value, move: lax.ppermute(value, AXES, pairs(move, x_size, z_size))
    dma = lambda n: pltpu.SemaphoreType.DMA((n,))

    piece = lambda n: shaped(n, 256, LEV)
    out_0 = pack(pack_first, shaped(256, 512), 1, 1, "pack_first")(covariance)
    pair_0 = send(out_0, swap_y)
    covariance, mix_a, mix_b, out_0 = lax.optimization_barrier((covariance, mix_a, mix_b, out_0))
    out_across, out_near, out_core = pack(
        pack_second, (shaped(6, LEV, LEV), piece(7), shaped(2, LEV, LEV)), 3, 11, "pack_second"
    )(covariance, mix_a, mix_b)
    across = send(out_across, functools.partial(mats_across, x_size))
    near = send(out_near, near_z)
    covariance, out_across = lax.optimization_barrier((covariance, out_across))
    out_1, out_far_1 = pack(pack_rest, (shaped(256, 512), piece(3)), 1, 4, "pack_rest")(covariance)
    pair_1 = send(out_1, swap_y)
    out_far_0 = pack(pack_far, piece(4), 2, 5, "pack_far")(pair_0, across)
    far_0 = send(out_far_0, far_z)
    far_1 = send(out_far_1, far_direct)

    weight = shaped(8, 256, 256, dtype=BF16)
    ends = shaped(4, 256, 256, dtype=BF16)
    prep_scratch = [pltpu.SMEM((2, 16), F32)]
    weights_b, coef_b = call(
        prepare_b, (weight, shaped(144)), [SMEM] * 3 + [VMEM] * 2, (VMEM, SMEM), prep_scratch, 10**3,
        "prepare_b",
    )(table, winds, barriers, across, mix_b)
    weights_b, far_0, pair_1 = lax.optimization_barrier((weights_b, far_0, pair_1))
    block = shaped(2, 512, LEV)
    field = pltpu.VMEM((WINDOW, 256, LEV), F32)
    kept_0, sent_0, ends_b = call(
        functools.partial(sweep_b, 0), (block, block, ends), [SMEM] + [VMEM] * 5, (VMEM,) * 3,
        [field, field], COST, "sweep_b0",
    )(coef_b, weights_b, covariance, pair_0, near, far_0)
    got_0 = send(sent_0, swap_y)
    kept_1, sent_1, out_same, out_cross = call(
        functools.partial(sweep_b, 1), (block, block, shaped(3, 512, LEV), shaped(3, 512, LEV)),
        [SMEM] + [VMEM] * 6 + [ANY, ANY], (VMEM, VMEM, ANY, ANY),
        [field, field, dma(4)], COST, "sweep_b1",
    )(coef_b, weights_b, covariance, pair_1, near, far_1, ends_b, kept_0, sent_0)
    got_1 = send(sent_1, swap_y)
    cross = send(out_cross, halo_cross)
    out_same, out_core, got_0 = lax.optimization_barrier((out_same, out_core, got_0))
    same = send(out_same, halo_same)
    core = send(out_core, mats_core)
    weights_a, ends_a, coef_a = call(
        prepare_a, (weight, ends, shaped(144)), [SMEM] * 3 + [VMEM] * 3, (VMEM, VMEM, SMEM),
        prep_scratch, 10**3, "prepare_a",
    )(table, winds, barriers, mix_a, across, core)
    got_0, weights_a = lax.optimization_barrier((got_0, weights_a))
    relay_0 = send(got_0, relay_core)
    relay_1 = send(got_1[1:], relay_core)

    field = pltpu.VMEM((WINDOW, 512, LEV), F32)
    return call(
        sweep_a, shaped(512, 1024), [SMEM] + [VMEM] * 7 + [ANY] * 3, VMEM, [field, field, dma(3)],
        4 * 10**3, "sweep_a",
    )(coef_a, weights_a, ends_a, kept_0, kept_1, got_0, got_1, same, cross, relay_0, relay_1)


def solution(mesh):
    placed = (P("row", "col"), P(), P(), P(), P("row", None, None), P("col", None, None))
    return jax.shard_map(
        functools.partial(per_device, mesh.shape["row"] // 4, mesh.shape["col"] // 2),
        mesh=mesh, in_specs=placed, out_specs=P("col", "row"), check_vma=False,
    )
```

```python
import functools
import itertools

import jax
import jax.numpy as jnp
from jax import lax
from jax.experimental import pallas as pl
from jax.experimental.pallas import tpu as pltpu
from jax.sharding import PartitionSpec as P

LAT = 128
LEV = 128
STEPS = 3
SPREAD = 0.15
WINDOW = 14
F32, BF16 = jnp.float32, jnp.bfloat16
COST = 4 * 10**9
AXES = ("row", "col")
ANY = pl.BlockSpec(memory_space=pl.ANY)
SMEM = pl.BlockSpec(memory_space=pltpu.SMEM)
VMEM = pl.BlockSpec(memory_space=pltpu.VMEM)


def pairs(move, x_size, z_size):
    number = lambda x, h, k, z, l: ((x * 2 + h) * 2 + k) * (2 * z_size) + z * 2 + l
    listed = []
    for x, h, k, z, l in itertools.product(range(x_size), range(2), range(2), range(z_size), range(2)):
        to = move(x, h, k, z, l)
        if to is not None and 0 <= to[0] < x_size and 0 <= to[3] < z_size:
            listed.append((number(x, h, k, z, l), number(*to)))
    return listed


def row_shift(x, h, k, by):
    at = (x * 2 + h) * 2 + k + by
    return at // 4, (at // 2) % 2, at % 2


def swap_y(x, h, k, z, l):
    return x, h, k, z, 1 - l


def near_z(x, h, k, z, l):
    return x, h, k, z + (1 if l else -1), l


def far_z(x, h, k, z, l):
    return x, h, k, z + (-1 if l else 1), l


def mats_across(size, x, h, k, z, l):
    tx, th, tk = row_shift(x, h, k, 1 if k else -1)
    return tx % size, th, tk, z, 1 - l


def mats_core(x, h, k, z, l):
    return x, h, 1 - k, z, l


def halo_same(x, h, k, z, l):
    return *row_shift(x, h, k, 1 if l else -1), z, l


def halo_cross(x, h, k, z, l):
    tx, th, tk = row_shift(x, h, k, 1 if l else -1)
    return None if (tx, th) == (x, h) else (tx, th, tk, z, 1 - l)


def relay_core(x, h, k, z, l):
    return (x, h, 1 - k, z, l) if k == l else None


def side():
    return lax.rem(lax.axis_index("col"), 2)


def turned(l, q, count):
    return jnp.where(l == 1, q, count - 1 - q)


def rows_of(l, chunk):
    return l * 768 if chunk == 0 else 256 + l * 256


def run_copies(copies, sems):
    started = []
    for i, (src, dst) in enumerate(copies):
        copy = pltpu.make_async_copy(src, dst, sems.at[i])
        copy.start()
        started.append(copy)
    for copy in started:
        copy.wait()


def lanes(start):
    return pl.ds(pl.multiple_of(start * LEV, LEV), LEV)


def rows(start, size):
    return pl.ds(pl.multiple_of(start, LEV), size)


def pack_first(cov, first, sems):
    run_copies([(cov.at[rows(rows_of(1 - side(), 0), 256)], first)], sems)


def pack_second(cov, mix_a, mix_b, across, near, core, sems):
    l = side()
    k = lax.rem(lax.axis_index("row"), 2)
    copies = [
        (mix_b, across.at[pl.ds(0, 4)]),
        (mix_a.at[pl.ds(6 * k, 2)], across.at[pl.ds(4, 2)]),
        (mix_a.at[pl.ds(6 - 6 * k, 2)], core),
    ]
    for c in range(2):
        for i in range(3):
            copies.append((cov.at[rows(rows_of(l, c), 256), lanes(l + i)], near.at[3 * c + i]))
    for m in range(2):
        copies.append((mix_b.at[2 * l + m], near.at[6, pl.ds(m * LEV, LEV)]))
    run_copies(copies, sems)


def pack_swap(cov, out, sems):
    run_copies([(cov.at[rows(rows_of(1 - side(), 1), 256)], out)], sems)


def pack_halo(pair, out, sems):
    l = side()
    run_copies([(pair.at[:, lanes(1 - l + i)], out.at[i]) for i in range(3)], sems)


def pack_far(pair, across, out, sems):
    l = side()
    copies = [(pair.at[:, lanes(1 - l + i)], out.at[i]) for i in range(3)]
    for m in range(2):
        copies.append((across.at[2 - 2 * l + m], out.at[3, pl.ds(m * LEV, LEV)]))
    run_copies(copies, sems)


def write_coefficients(l, base, tracer, table, winds, barriers, coef, flow):
    def interface(step, n):
        g = base + n - 3
        inside = (g >= 1) & (g <= LAT - 1)
        c = table[winds[tracer, step], jnp.clip(g, 0, LAT - 1)]
        blocked = barriers[0] == g
        for b in range(1, 4):
            blocked = blocked | (barriers[b] == g)
        c = c * jnp.where(blocked, 0.25, 1.0)
        flow[0, n] = jnp.where(inside, jnp.maximum(c, 0.0) + SPREAD, 0.0)
        flow[1, n] = jnp.where(inside, jnp.maximum(-c, 0.0) + SPREAD, 0.0)

    for step in range(STEPS):
        lax.fori_loop(0, WINDOW + 1, lambda n, _: interface(step, n), None)

        def place(p, _):
            n = turned(l, p, WINDOW)
            below, above = flow[0, n], flow[1, n + 1]
            coef[step * 48 + p] = jnp.where(l == 1, below, above)
            coef[step * 48 + 16 + p] = 1.0 - flow[1, n] - flow[0, n + 1]
            coef[step * 48 + 32 + p] = jnp.where(l == 1, above, below)

        lax.fori_loop(0, WINDOW, place, None)


def write_weight(weights, at, mixer):
    turned_mixer = mixer.T
    high = turned_mixer.astype(BF16)
    low = (turned_mixer - high.astype(F32)).astype(BF16)
    for half in range(2):
        weights[at, half * LEV : (half + 1) * LEV, :LEV] = high
        weights[at, half * LEV : (half + 1) * LEV, LEV:] = low


def prepare_b(table, winds, barriers, across, own, weights, coef, flow):
    l = side()
    base = lax.axis_index("col") // 2 * 8
    write_coefficients(l, base, 1, table, winds, barriers, coef, flow)
    for q in range(4):
        b = turned(l, q, 4)
        write_weight(weights, q, across[b])
        write_weight(weights, 4 + q, own[b])


def prepare_a(table, winds, barriers, own, across, core, weights, ends, coef, flow):
    l = side()
    k = lax.rem(lax.axis_index("row"), 2)
    base = lax.axis_index("row") * 8
    write_coefficients(l, base, 0, table, winds, barriers, coef, flow)
    for q in range(8):
        write_weight(weights, q, own[turned(l, q, 8)])
    for q in range(2):
        m = turned(l, q, 2)
        write_weight(ends, q, jnp.where(k == l, core[m], across[4 + m]))
        write_weight(ends, 2 + q, jnp.where(k == l, across[4 + m], core[m]))


def step_latitude(step, p, source, weights, ends, coef):
    weight = weights[p - 3] if 3 <= p <= 10 else ends[p - 1 if p < 3 else p - 9]
    y = (
        coef[step * 48 + p] * source(p - 1)
        + coef[step * 48 + 16 + p] * source(p)
        + coef[step * 48 + 32 + p] * source(p + 1)
    )
    high = y.astype(BF16)
    low = (y - high.astype(F32)).astype(BF16)
    both = jnp.dot(
        jnp.concatenate([high, low], axis=1), weight, preferred_element_type=F32
    )
    return both[:, :LEV] + both[:, LEV:]


def first_steps(source, window, other, weights, ends, coef):
    for p in range(1, WINDOW - 1):
        other[p] = step_latitude(0, p, source, weights, ends, coef)
    for p in range(2, WINDOW - 2):
        window[p] = step_latitude(1, p, lambda at: other[at], weights, ends, coef)


def sweep_b(chunk, *refs):
    if chunk == 0:
        coef, weights, cov, pair, near, far, kept, sent, ends, window, other = refs
    else:
        (coef, weights, cov, pair, near, far, ends, kept_before, sent_before,
         kept, sent, same, cross, window, other, late) = refs
    l = side()

    def source(p):
        if p < 3:
            return near[3 * chunk + turned(l, p, 3)]
        if p < 7:
            return pair[:, lanes(turned(l, p - 3, 4))]
        if p < 11:
            return cov[rows(rows_of(l, chunk), 256), lanes(turned(l, p - 7, 4))]
        return far[turned(l, p - 11, 3)]

    if chunk == 0:
        for q in range(2):
            at = rows(turned(l, q, 2) * LEV, LEV)
            write_weight(ends, q, near[6, at, :])
            write_weight(ends, 2 + q, far[3, at, :])
    first_steps(source, window, other, weights, ends, coef)

    def finish(p, target, q):
        z = step_latitude(2, p, lambda at: window[at], weights, ends, coef)
        b = turned(l, q, 4)
        for i in range(2):
            u = turned(l, i, 2)
            target[u, rows(b * LEV, LEV), :] = z[i * LEV : (i + 1) * LEV].T

    for q in range(4):
        finish(3 + q, sent, q)
    for q in range(4):
        finish(7 + q, kept, q)
    if chunk == 1:
        run_copies(
            [
                (kept_before, same.at[pl.ds(1, 2)]),
                (sent_before, cross.at[pl.ds(1, 2)]),
                (kept.at[1], same.at[0]),
                (sent.at[1], cross.at[0]),
            ],
            late,
        )


def sweep_a(coef, weights, ends, kept_0, kept_1, got_0, got_1, same, cross, relay_0, relay_1, out,
            window, other, sems):
    l = side()
    k = lax.rem(lax.axis_index("row"), 2)

    @pl.when(k == l)
    def _():
        run_copies([(cross.at[q], window.at[13 - q]) for q in range(3)], sems)

    @pl.when(k != l)
    def _():
        copies = [(relay_0.at[u], window.at[12 - u]) for u in range(2)]
        run_copies(copies + [(relay_1.at[0], window.at[13])], sems)

    def source(p):
        if p < 3:
            return same[p]
        if p < 7:
            return (got_0, got_1)[p > 4][p % 2 if p > 4 else 4 - p]
        if p < 11:
            return (kept_1, kept_0)[p > 8][1 - p % 2]
        return window[p]

    first_steps(source, window, other, weights, ends, coef)
    for p in range(3, WINDOW - 3):
        out[:, lanes(turned(l, p - 3, 8))] = step_latitude(
            2, p, lambda at: window[at], weights, ends, coef
        )


def pack(kernel, outs, operands, copies, name):
    return pl.pallas_call(
        kernel,
        out_shape=outs,
        in_specs=[ANY] * operands,
        out_specs=ANY if isinstance(outs, jax.ShapeDtypeStruct) else (ANY,) * len(outs),
        scratch_shapes=[pltpu.SemaphoreType.DMA((copies,))],
        compiler_params=pltpu.CompilerParams(vmem_limit_bytes=40 * 1024 * 1024),
        cost_estimate=pl.CostEstimate(flops=0, bytes_accessed=2**10, transcendentals=0),
        name=name,
    )


def call(kernel, outs, in_specs, out_specs, scratch, flops, name):
    return pl.pallas_call(
        kernel,
        out_shape=outs,
        in_specs=in_specs,
        out_specs=out_specs,
        scratch_shapes=scratch,
        compiler_params=pltpu.CompilerParams(vmem_limit_bytes=40 * 1024 * 1024),
        cost_estimate=pl.CostEstimate(flops=flops, bytes_accessed=2**10, transcendentals=0),
        name=name,
    )


def shaped(*dims, dtype=F32):
    return jax.ShapeDtypeStruct(dims, dtype)


def per_device(x_size, z_size, covariance, table, winds, barriers, mix_a, mix_b):
    send = lambda value, move: lax.ppermute(value, AXES, pairs(move, x_size, z_size))
    dma = lambda n: pltpu.SemaphoreType.DMA((n,))

    piece = lambda n: shaped(n, 256, LEV)
    out_0 = pack(pack_first, shaped(256, 512), 1, 1, "pack_first")(covariance)
    pair_0 = send(out_0, swap_y)
    covariance, mix_a, mix_b, out_0 = lax.optimization_barrier((covariance, mix_a, mix_b, out_0))
    out_across, out_near, out_core = pack(
        pack_second, (shaped(6, LEV, LEV), piece(7), shaped(2, LEV, LEV)), 3, 11, "pack_second"
    )(covariance, mix_a, mix_b)
    across = send(out_across, functools.partial(mats_across, x_size))
    near = send(out_near, near_z)
    covariance, out_across = lax.optimization_barrier((covariance, out_across))
    out_1 = pack(pack_swap, shaped(256, 512), 1, 1, "pack_swap")(covariance)
    pair_1 = send(out_1, swap_y)
    out_far_0 = pack(pack_far, piece(4), 2, 5, "pack_far")(pair_0, across)
    far_0 = send(out_far_0, far_z)
    out_far_1 = pack(pack_halo, piece(3), 1, 3, "pack_halo")(pair_1)

    weight = shaped(8, 256, 256, dtype=BF16)
    ends = shaped(4, 256, 256, dtype=BF16)
    prep_scratch = [pltpu.SMEM((2, 16), F32)]
    weights_b, coef_b = call(
        prepare_b, (weight, shaped(144)), [SMEM] * 3 + [VMEM] * 2, (VMEM, SMEM), prep_scratch, 10**3,
        "prepare_b",
    )(table, winds, barriers, across, mix_b)
    far_1 = send(out_far_1, far_z)
    weights_b, far_0, out_far_1 = lax.optimization_barrier((weights_b, far_0, out_far_1))
    block = shaped(2, 512, LEV)
    field = pltpu.VMEM((WINDOW, 256, LEV), F32)
    kept_0, sent_0, ends_b = call(
        functools.partial(sweep_b, 0), (block, block, ends), [SMEM] + [VMEM] * 5, (VMEM,) * 3,
        [field, field], COST, "sweep_b0",
    )(coef_b, weights_b, covariance, pair_0, near, far_0)
    got_0 = send(sent_0, swap_y)
    kept_1, sent_1, out_same, out_cross = call(
        functools.partial(sweep_b, 1), (block, block, shaped(3, 512, LEV), shaped(3, 512, LEV)),
        [SMEM] + [VMEM] * 6 + [ANY, ANY], (VMEM, VMEM, ANY, ANY),
        [field, field, dma(4)], COST, "sweep_b1",
    )(coef_b, weights_b, covariance, pair_1, near, far_1, ends_b, kept_0, sent_0)
    got_1 = send(sent_1, swap_y)
    cross = send(out_cross, halo_cross)
    out_same, out_core, got_0 = lax.optimization_barrier((out_same, out_core, got_0))
    same = send(out_same, halo_same)
    core = send(out_core, mats_core)
    weights_a, ends_a, coef_a = call(
        prepare_a, (weight, ends, shaped(144)), [SMEM] * 3 + [VMEM] * 3, (VMEM, VMEM, SMEM),
        prep_scratch, 10**3, "prepare_a",
    )(table, winds, barriers, mix_a, across, core)
    got_0, weights_a = lax.optimization_barrier((got_0, weights_a))
    relay_0 = send(got_0, relay_core)
    relay_1 = send(got_1[1:], relay_core)

    field = pltpu.VMEM((WINDOW, 512, LEV), F32)
    return call(
        sweep_a, shaped(512, 1024), [SMEM] + [VMEM] * 7 + [ANY] * 3, VMEM, [field, field, dma(3)],
        4 * 10**3, "sweep_a",
    )(coef_a, weights_a, ends_a, kept_0, kept_1, got_0, got_1, same, cross, relay_0, relay_1)


def solution(mesh):
    placed = (P("row", "col"), P(), P(), P(), P("row", None, None), P("col", None, None))
    return jax.shard_map(
        functools.partial(per_device, mesh.shape["row"] // 4, mesh.shape["col"] // 2),
        mesh=mesh, in_specs=placed, out_specs=P("col", "row"), check_vma=False,
    )
```

```python
import functools
import itertools

import jax
import jax.numpy as jnp
from jax import lax
from jax.experimental import pallas as pl
from jax.experimental.pallas import tpu as pltpu
from jax.sharding import PartitionSpec as P

LAT = 128
LEV = 128
STEPS = 3
SPREAD = 0.15
WINDOW = 14
F32, BF16 = jnp.float32, jnp.bfloat16
COST = 4 * 10**9
AXES = ("row", "col")
ANY = pl.BlockSpec(memory_space=pl.ANY)
SMEM = pl.BlockSpec(memory_space=pltpu.SMEM)
VMEM = pl.BlockSpec(memory_space=pltpu.VMEM)


def pairs(move, x_size, z_size):
    number = lambda x, h, k, z, l: ((x * 2 + h) * 2 + k) * (2 * z_size) + z * 2 + l
    listed = []
    for x, h, k, z, l in itertools.product(range(x_size), range(2), range(2), range(z_size), range(2)):
        to = move(x, h, k, z, l)
        if to is not None and 0 <= to[0] < x_size and 0 <= to[3] < z_size:
            listed.append((number(x, h, k, z, l), number(*to)))
    return listed


def row_shift(x, h, k, by):
    at = (x * 2 + h) * 2 + k + by
    return at // 4, (at // 2) % 2, at % 2


def swap_y(x, h, k, z, l):
    return x, h, k, z, 1 - l


def near_z(x, h, k, z, l):
    return x, h, k, z + (1 if l else -1), l


def far_z(x, h, k, z, l):
    return x, h, k, z + (-1 if l else 1), l


def mats_across(size, x, h, k, z, l):
    tx, th, tk = row_shift(x, h, k, 1 if k else -1)
    return tx % size, th, tk, z, 1 - l


def mats_core(x, h, k, z, l):
    return x, h, 1 - k, z, l


def halo_same(x, h, k, z, l):
    return *row_shift(x, h, k, 1 if l else -1), z, l


def halo_cross(x, h, k, z, l):
    tx, th, tk = row_shift(x, h, k, 1 if l else -1)
    return None if (tx, th) == (x, h) else (tx, th, tk, z, 1 - l)


def relay_core(x, h, k, z, l):
    return (x, h, 1 - k, z, l) if k == l else None


def side():
    return lax.rem(lax.axis_index("col"), 2)


def turned(l, q, count):
    return jnp.where(l == 1, q, count - 1 - q)


def rows_of(l, chunk):
    return l * 768 if chunk == 0 else 256 + l * 256


def run_copies(copies, sems):
    started = []
    for i, (src, dst) in enumerate(copies):
        copy = pltpu.make_async_copy(src, dst, sems.at[i])
        copy.start()
        started.append(copy)
    for copy in started:
        copy.wait()


def lanes(start):
    return pl.ds(pl.multiple_of(start * LEV, LEV), LEV)


def rows(start, size):
    return pl.ds(pl.multiple_of(start, LEV), size)


def pack_first(cov, first, sems):
    run_copies([(cov.at[rows(rows_of(1 - side(), 0), 256)], first)], sems)


def pack_second(cov, mix_a, mix_b, across, near, core, sems):
    l = side()
    k = lax.rem(lax.axis_index("row"), 2)
    copies = [
        (mix_b, across.at[pl.ds(0, 4)]),
        (mix_a.at[pl.ds(6 * k, 2)], across.at[pl.ds(4, 2)]),
        (mix_a.at[pl.ds(6 - 6 * k, 2)], core),
    ]
    for c in range(2):
        for i in range(3):
            copies.append((cov.at[rows(rows_of(l, c), 256), lanes(l + i)], near.at[3 * c + i]))
    for m in range(2):
        copies.append((mix_b.at[2 * l + m], near.at[6, pl.ds(m * LEV, LEV)]))
    run_copies(copies, sems)


def pack_swap(cov, out, sems):
    run_copies([(cov.at[rows(rows_of(1 - side(), 1), 256)], out)], sems)


def pack_halo(pair, out, sems):
    l = side()
    run_copies([(pair.at[:, lanes(1 - l + i)], out.at[i]) for i in range(3)], sems)


def pack_edge(across, out, sems):
    run_copies([(across.at[pl.ds(2 - 2 * side(), 2)], out)], sems)


def write_coefficients(l, base, tracer, table, winds, barriers, coef, flow):
    def interface(step, n):
        g = base + n - 3
        inside = (g >= 1) & (g <= LAT - 1)
        c = table[winds[tracer, step], jnp.clip(g, 0, LAT - 1)]
        blocked = barriers[0] == g
        for b in range(1, 4):
            blocked = blocked | (barriers[b] == g)
        c = c * jnp.where(blocked, 0.25, 1.0)
        flow[0, n] = jnp.where(inside, jnp.maximum(c, 0.0) + SPREAD, 0.0)
        flow[1, n] = jnp.where(inside, jnp.maximum(-c, 0.0) + SPREAD, 0.0)

    for step in range(STEPS):
        lax.fori_loop(0, WINDOW + 1, lambda n, _: interface(step, n), None)

        def place(p, _):
            n = turned(l, p, WINDOW)
            below, above = flow[0, n], flow[1, n + 1]
            coef[step * 48 + p] = jnp.where(l == 1, below, above)
            coef[step * 48 + 16 + p] = 1.0 - flow[1, n] - flow[0, n + 1]
            coef[step * 48 + 32 + p] = jnp.where(l == 1, above, below)

        lax.fori_loop(0, WINDOW, place, None)


def write_weight(weights, at, mixer):
    turned_mixer = mixer.T
    high = turned_mixer.astype(BF16)
    low = (turned_mixer - high.astype(F32)).astype(BF16)
    for half in range(2):
        weights[at, half * LEV : (half + 1) * LEV, :LEV] = high
        weights[at, half * LEV : (half + 1) * LEV, LEV:] = low


def prepare_b(table, winds, barriers, across, own, weights, coef, flow):
    l = side()
    base = lax.axis_index("col") // 2 * 8
    write_coefficients(l, base, 1, table, winds, barriers, coef, flow)
    for q in range(4):
        b = turned(l, q, 4)
        write_weight(weights, q, across[b])
        write_weight(weights, 4 + q, own[b])


def prepare_a(table, winds, barriers, own, across, core, weights, ends, coef, flow):
    l = side()
    k = lax.rem(lax.axis_index("row"), 2)
    base = lax.axis_index("row") * 8
    write_coefficients(l, base, 0, table, winds, barriers, coef, flow)
    for q in range(8):
        write_weight(weights, q, own[turned(l, q, 8)])
    for q in range(2):
        m = turned(l, q, 2)
        write_weight(ends, q, jnp.where(k == l, core[m], across[4 + m]))
        write_weight(ends, 2 + q, jnp.where(k == l, across[4 + m], core[m]))


def step_latitude(step, p, source, weights, ends, coef):
    weight = weights[p - 3] if 3 <= p <= 10 else ends[p - 1 if p < 3 else p - 9]
    y = (
        coef[step * 48 + p] * source(p - 1)
        + coef[step * 48 + 16 + p] * source(p)
        + coef[step * 48 + 32 + p] * source(p + 1)
    )
    high = y.astype(BF16)
    low = (y - high.astype(F32)).astype(BF16)
    both = jnp.dot(
        jnp.concatenate([high, low], axis=1), weight, preferred_element_type=F32
    )
    return both[:, :LEV] + both[:, LEV:]


def first_steps(source, window, other, weights, ends, coef):
    for p in range(1, WINDOW - 1):
        other[p] = step_latitude(0, p, source, weights, ends, coef)
    for p in range(2, WINDOW - 2):
        window[p] = step_latitude(1, p, lambda at: other[at], weights, ends, coef)


def sweep_b(chunk, *refs):
    if chunk == 0:
        coef, weights, cov, pair, near, far, edge, kept, sent, ends, window, other = refs
    else:
        (coef, weights, cov, pair, near, far, ends, kept_before, sent_before,
         kept, sent, same, cross, window, other, late) = refs
    l = side()

    def source(p):
        if p < 3:
            return near[3 * chunk + turned(l, p, 3)]
        if p < 7:
            return pair[:, lanes(turned(l, p - 3, 4))]
        if p < 11:
            return cov[rows(rows_of(l, chunk), 256), lanes(turned(l, p - 7, 4))]
        return far[turned(l, p - 11, 3)]

    if chunk == 0:
        for q in range(2):
            m = turned(l, q, 2)
            write_weight(ends, q, near[6, rows(m * LEV, LEV), :])
            write_weight(ends, 2 + q, edge[m])
    first_steps(source, window, other, weights, ends, coef)

    def finish(p, target, q):
        z = step_latitude(2, p, lambda at: window[at], weights, ends, coef)
        b = turned(l, q, 4)
        for i in range(2):
            u = turned(l, i, 2)
            target[u, rows(b * LEV, LEV), :] = z[i * LEV : (i + 1) * LEV].T

    for q in range(4):
        finish(3 + q, sent, q)
    for q in range(4):
        finish(7 + q, kept, q)
    if chunk == 1:
        run_copies(
            [
                (kept_before, same.at[pl.ds(1, 2)]),
                (sent_before, cross.at[pl.ds(1, 2)]),
                (kept.at[1], same.at[0]),
                (sent.at[1], cross.at[0]),
            ],
            late,
        )


def sweep_a(coef, weights, ends, kept_0, kept_1, got_0, got_1, same, cross, relay_0, relay_1, out,
            window, other, sems):
    l = side()
    k = lax.rem(lax.axis_index("row"), 2)

    @pl.when(k == l)
    def _():
        run_copies([(cross.at[q], window.at[13 - q]) for q in range(3)], sems)

    @pl.when(k != l)
    def _():
        copies = [(relay_0.at[u], window.at[12 - u]) for u in range(2)]
        run_copies(copies + [(relay_1.at[0], window.at[13])], sems)

    def source(p):
        if p < 3:
            return same[p]
        if p < 7:
            return (got_0, got_1)[p > 4][p % 2 if p > 4 else 4 - p]
        if p < 11:
            return (kept_1, kept_0)[p > 8][1 - p % 2]
        return window[p]

    first_steps(source, window, other, weights, ends, coef)
    for p in range(3, WINDOW - 3):
        out[:, lanes(turned(l, p - 3, 8))] = step_latitude(
            2, p, lambda at: window[at], weights, ends, coef
        )


def pack(kernel, outs, operands, copies, name):
    return pl.pallas_call(
        kernel,
        out_shape=outs,
        in_specs=[ANY] * operands,
        out_specs=ANY if isinstance(outs, jax.ShapeDtypeStruct) else (ANY,) * len(outs),
        scratch_shapes=[pltpu.SemaphoreType.DMA((copies,))],
        compiler_params=pltpu.CompilerParams(vmem_limit_bytes=40 * 1024 * 1024),
        cost_estimate=pl.CostEstimate(flops=0, bytes_accessed=2**10, transcendentals=0),
        name=name,
    )


def call(kernel, outs, in_specs, out_specs, scratch, flops, name):
    return pl.pallas_call(
        kernel,
        out_shape=outs,
        in_specs=in_specs,
        out_specs=out_specs,
        scratch_shapes=scratch,
        compiler_params=pltpu.CompilerParams(vmem_limit_bytes=40 * 1024 * 1024),
        cost_estimate=pl.CostEstimate(flops=flops, bytes_accessed=2**10, transcendentals=0),
        name=name,
    )


def shaped(*dims, dtype=F32):
    return jax.ShapeDtypeStruct(dims, dtype)


def per_device(x_size, z_size, covariance, table, winds, barriers, mix_a, mix_b):
    send = lambda value, move: lax.ppermute(value, AXES, pairs(move, x_size, z_size))
    dma = lambda n: pltpu.SemaphoreType.DMA((n,))

    piece = lambda n: shaped(n, 256, LEV)
    out_0 = pack(pack_first, shaped(256, 512), 1, 1, "pack_first")(covariance)
    pair_0 = send(out_0, swap_y)
    covariance, mix_a, mix_b, out_0 = lax.optimization_barrier((covariance, mix_a, mix_b, out_0))
    out_across, out_near, out_core = pack(
        pack_second, (shaped(6, LEV, LEV), piece(7), shaped(2, LEV, LEV)), 3, 11, "pack_second"
    )(covariance, mix_a, mix_b)
    across = send(out_across, functools.partial(mats_across, x_size))
    near = send(out_near, near_z)
    covariance, out_across = lax.optimization_barrier((covariance, out_across))
    out_1 = pack(pack_swap, shaped(256, 512), 1, 1, "pack_swap")(covariance)
    pair_1 = send(out_1, swap_y)
    pair_0, across = lax.optimization_barrier((pair_0, across))
    far_0 = send(pack(pack_halo, piece(3), 1, 3, "pack_halo")(pair_0), far_z)
    edge_far = send(pack(pack_edge, shaped(2, LEV, LEV), 1, 1, "pack_edge")(across), far_z)

    weight = shaped(8, 256, 256, dtype=BF16)
    ends = shaped(4, 256, 256, dtype=BF16)
    prep_scratch = [pltpu.SMEM((2, 16), F32)]
    weights_b, coef_b = call(
        prepare_b, (weight, shaped(144)), [SMEM] * 3 + [VMEM] * 2, (VMEM, SMEM), prep_scratch, 10**3,
        "prepare_b",
    )(table, winds, barriers, across, mix_b)
    pair_1, weights_b = lax.optimization_barrier((pair_1, weights_b))
    out_far_1 = pack(pack_halo, piece(3), 1, 3, "pack_halo")(pair_1)
    far_1 = send(out_far_1, far_z)
    weights_b, far_0, out_far_1 = lax.optimization_barrier((weights_b, far_0, out_far_1))
    block = shaped(2, 512, LEV)
    field = pltpu.VMEM((WINDOW, 256, LEV), F32)
    kept_0, sent_0, ends_b = call(
        functools.partial(sweep_b, 0), (block, block, ends), [SMEM] + [VMEM] * 6, (VMEM,) * 3,
        [field, field], COST, "sweep_b0",
    )(coef_b, weights_b, covariance, pair_0, near, far_0, edge_far)
    got_0 = send(sent_0, swap_y)
    kept_1, sent_1, out_same, out_cross = call(
        functools.partial(sweep_b, 1), (block, block, shaped(3, 512, LEV), shaped(3, 512, LEV)),
        [SMEM] + [VMEM] * 6 + [ANY, ANY], (VMEM, VMEM, ANY, ANY),
        [field, field, dma(4)], COST, "sweep_b1",
    )(coef_b, weights_b, covariance, pair_1, near, far_1, ends_b, kept_0, sent_0)
    got_1 = send(sent_1, swap_y)
    cross = send(out_cross, halo_cross)
    out_same, out_core, got_0 = lax.optimization_barrier((out_same, out_core, got_0))
    same = send(out_same, halo_same)
    core = send(out_core, mats_core)
    weights_a, ends_a, coef_a = call(
        prepare_a, (weight, ends, shaped(144)), [SMEM] * 3 + [VMEM] * 3, (VMEM, VMEM, SMEM),
        prep_scratch, 10**3, "prepare_a",
    )(table, winds, barriers, mix_a, across, core)
    got_0, weights_a = lax.optimization_barrier((got_0, weights_a))
    relay_0 = send(got_0, relay_core)
    relay_1 = send(got_1[1:], relay_core)

    field = pltpu.VMEM((WINDOW, 512, LEV), F32)
    return call(
        sweep_a, shaped(512, 1024), [SMEM] + [VMEM] * 7 + [ANY] * 3, VMEM, [field, field, dma(3)],
        4 * 10**3, "sweep_a",
    )(coef_a, weights_a, ends_a, kept_0, kept_1, got_0, got_1, same, cross, relay_0, relay_1)


def solution(mesh):
    placed = (P("row", "col"), P(), P(), P(), P("row", None, None), P("col", None, None))
    return jax.shard_map(
        functools.partial(per_device, mesh.shape["row"] // 4, mesh.shape["col"] // 2),
        mesh=mesh, in_specs=placed, out_specs=P("col", "row"), check_vma=False,
    )
```

```python
import functools
import itertools

import jax
import jax.numpy as jnp
from jax import lax
from jax.experimental import pallas as pl
from jax.experimental.pallas import tpu as pltpu
from jax.sharding import PartitionSpec as P

LAT = 128
LEV = 128
STEPS = 3
SPREAD = 0.15
WINDOW = 14
F32, BF16 = jnp.float32, jnp.bfloat16
COST = 4 * 10**9
AXES = ("row", "col")
ANY = pl.BlockSpec(memory_space=pl.ANY)
SMEM = pl.BlockSpec(memory_space=pltpu.SMEM)
VMEM = pl.BlockSpec(memory_space=pltpu.VMEM)


def pairs(move, x_size, z_size):
    number = lambda x, h, k, z, l: ((x * 2 + h) * 2 + k) * (2 * z_size) + z * 2 + l
    listed = []
    for x, h, k, z, l in itertools.product(range(x_size), range(2), range(2), range(z_size), range(2)):
        to = move(x, h, k, z, l)
        if to is not None and 0 <= to[0] < x_size and 0 <= to[3] < z_size:
            listed.append((number(x, h, k, z, l), number(*to)))
    return listed


def row_shift(x, h, k, by):
    at = (x * 2 + h) * 2 + k + by
    return at // 4, (at // 2) % 2, at % 2


def swap_y(x, h, k, z, l):
    return x, h, k, z, 1 - l


def near_z(x, h, k, z, l):
    return x, h, k, z + (1 if l else -1), l


def far_z(x, h, k, z, l):
    return x, h, k, z + (-1 if l else 1), l


def mats_across(size, x, h, k, z, l):
    tx, th, tk = row_shift(x, h, k, 1 if k else -1)
    return tx % size, th, tk, z, 1 - l


def mats_core(x, h, k, z, l):
    return x, h, 1 - k, z, l


def halo_same(x, h, k, z, l):
    return *row_shift(x, h, k, 1 if l else -1), z, l


def halo_cross(x, h, k, z, l):
    tx, th, tk = row_shift(x, h, k, 1 if l else -1)
    return None if (tx, th) == (x, h) else (tx, th, tk, z, 1 - l)


def relay_core(x, h, k, z, l):
    return (x, h, 1 - k, z, l) if k == l else None


def side():
    return lax.rem(lax.axis_index("col"), 2)


def turned(l, q, count):
    return jnp.where(l == 1, q, count - 1 - q)


def rows_of(l, chunk):
    return l * 768 if chunk == 0 else 256 + l * 256


def run_copies(copies, sems):
    started = []
    for i, (src, dst) in enumerate(copies):
        copy = pltpu.make_async_copy(src, dst, sems.at[i])
        copy.start()
        started.append(copy)
    for copy in started:
        copy.wait()


def lanes(start):
    return pl.ds(pl.multiple_of(start * LEV, LEV), LEV)


def rows(start, size):
    return pl.ds(pl.multiple_of(start, LEV), size)


def pack_first(cov, first, sems):
    run_copies([(cov.at[rows(rows_of(1 - side(), 0), 256)], first)], sems)


def pack_second(cov, mix_a, mix_b, across, near, core, sems):
    l = side()
    k = lax.rem(lax.axis_index("row"), 2)
    copies = [
        (mix_b, across.at[pl.ds(0, 4)]),
        (mix_a.at[pl.ds(6 * k, 2)], across.at[pl.ds(4, 2)]),
        (mix_a.at[pl.ds(6 - 6 * k, 2)], core),
    ]
    for c in range(2):
        for i in range(3):
            copies.append((cov.at[rows(rows_of(l, c), 256), lanes(l + i)], near.at[3 * c + i]))
    for m in range(2):
        copies.append((mix_b.at[2 * l + m], near.at[6, pl.ds(m * LEV, LEV)]))
    run_copies(copies, sems)


def pack_swap(cov, out, sems):
    run_copies([(cov.at[rows(rows_of(1 - side(), 1), 256)], out)], sems)


def pack_halo(pair, out, sems):
    l = side()
    run_copies([(pair.at[:, lanes(1 - l + i)], out.at[i]) for i in range(3)], sems)


def pack_far(pair, across, out, sems):
    l = side()
    copies = [(pair.at[:, lanes(1 - l + i)], out.at[i]) for i in range(3)]
    for m in range(2):
        copies.append((across.at[2 - 2 * l + m], out.at[3, pl.ds(m * LEV, LEV)]))
    run_copies(copies, sems)


def write_coefficients(l, base, tracer, table, winds, barriers, coef, flow):
    def interface(step, n):
        g = base + n - 3
        inside = (g >= 1) & (g <= LAT - 1)
        c = table[winds[tracer, step], jnp.clip(g, 0, LAT - 1)]
        blocked = barriers[0] == g
        for b in range(1, 4):
            blocked = blocked | (barriers[b] == g)
        c = c * jnp.where(blocked, 0.25, 1.0)
        flow[0, n] = jnp.where(inside, jnp.maximum(c, 0.0) + SPREAD, 0.0)
        flow[1, n] = jnp.where(inside, jnp.maximum(-c, 0.0) + SPREAD, 0.0)

    for step in range(STEPS):
        lax.fori_loop(0, WINDOW + 1, lambda n, _: interface(step, n), None)

        def place(p, _):
            n = turned(l, p, WINDOW)
            below, above = flow[0, n], flow[1, n + 1]
            coef[step * 48 + p] = jnp.where(l == 1, below, above)
            coef[step * 48 + 16 + p] = 1.0 - flow[1, n] - flow[0, n + 1]
            coef[step * 48 + 32 + p] = jnp.where(l == 1, above, below)

        lax.fori_loop(0, WINDOW, place, None)


def write_weight(weights, at, mixer):
    turned_mixer = mixer.T
    high = turned_mixer.astype(BF16)
    low = (turned_mixer - high.astype(F32)).astype(BF16)
    for half in range(2):
        weights[at, half * LEV : (half + 1) * LEV, :LEV] = high
        weights[at, half * LEV : (half + 1) * LEV, LEV:] = low


def prepare_b(table, winds, barriers, across, own, weights, coef, flow):
    l = side()
    base = lax.axis_index("col") // 2 * 8
    write_coefficients(l, base, 1, table, winds, barriers, coef, flow)
    for q in range(4):
        b = turned(l, q, 4)
        write_weight(weights, q, across[b])
        write_weight(weights, 4 + q, own[b])


def prepare_a(table, winds, barriers, own, across, core, weights, ends, coef, flow):
    l = side()
    k = lax.rem(lax.axis_index("row"), 2)
    base = lax.axis_index("row") * 8
    write_coefficients(l, base, 0, table, winds, barriers, coef, flow)
    for q in range(8):
        write_weight(weights, q, own[turned(l, q, 8)])
    for q in range(2):
        m = turned(l, q, 2)
        write_weight(ends, q, jnp.where(k == l, core[m], across[4 + m]))
        write_weight(ends, 2 + q, jnp.where(k == l, across[4 + m], core[m]))


def step_latitude(step, p, source, weights, ends, coef):
    weight = weights[p - 3] if 3 <= p <= 10 else ends[p - 1 if p < 3 else p - 9]
    y = (
        coef[step * 48 + p] * source(p - 1)
        + coef[step * 48 + 16 + p] * source(p)
        + coef[step * 48 + 32 + p] * source(p + 1)
    )
    high = y.astype(BF16)
    low = (y - high.astype(F32)).astype(BF16)
    both = jnp.dot(
        jnp.concatenate([high, low], axis=1), weight, preferred_element_type=F32
    )
    return both[:, :LEV] + both[:, LEV:]


def first_steps(source, window, other, weights, ends, coef):
    for p in range(1, WINDOW - 1):
        other[p] = step_latitude(0, p, source, weights, ends, coef)
    for p in range(2, WINDOW - 2):
        window[p] = step_latitude(1, p, lambda at: other[at], weights, ends, coef)


def sweep_b(chunk, *refs):
    if chunk == 0:
        coef, weights, cov, pair, near, far, kept, sent, ends, window, other = refs
    else:
        (coef, weights, cov, pair, near, far, ends, kept_before, sent_before,
         kept, sent, same, cross, window, other, late) = refs
    l = side()

    def source(p):
        if p < 3:
            return near[3 * chunk + turned(l, p, 3)]
        if p < 7:
            return pair[:, lanes(turned(l, p - 3, 4))]
        if p < 11:
            return cov[rows(rows_of(l, chunk), 256), lanes(turned(l, p - 7, 4))]
        return far[turned(l, p - 11, 3)]

    if chunk == 0:
        for q in range(2):
            at = rows(turned(l, q, 2) * LEV, LEV)
            write_weight(ends, q, near[6, at, :])
            write_weight(ends, 2 + q, far[3, at, :])
    first_steps(source, window, other, weights, ends, coef)

    def finish(p, target, q):
        z = step_latitude(2, p, lambda at: window[at], weights, ends, coef)
        b = turned(l, q, 4)
        for i in range(2):
            u = turned(l, i, 2)
            target[u, rows(b * LEV, LEV), :] = z[i * LEV : (i + 1) * LEV].T

    for q in range(4):
        finish(3 + q, sent, q)
    for q in range(4):
        finish(7 + q, kept, q)
    if chunk == 1:
        run_copies(
            [
                (kept_before, same.at[pl.ds(1, 2)]),
                (sent_before, cross.at[pl.ds(1, 2)]),
                (kept.at[1], same.at[0]),
                (sent.at[1], cross.at[0]),
            ],
            late,
        )


def sweep_a(coef, weights, ends, kept_0, kept_1, got_0, got_1, same, cross, relay_0, relay_1, out,
            window, other):
    l = side()
    k = lax.rem(lax.axis_index("row"), 2)

    def source(p):
        if p < 3:
            return same[p]
        if p < 7:
            return (got_0, got_1)[p > 4][p % 2 if p > 4 else 4 - p]
        if p < 11:
            return (kept_1, kept_0)[p > 8][1 - p % 2]
        relayed = relay_1[0] if p == 13 else relay_0[12 - p]
        return jnp.where(k == l, cross[13 - p], relayed)

    first_steps(source, window, other, weights, ends, coef)
    for p in range(3, WINDOW - 3):
        out[:, lanes(turned(l, p - 3, 8))] = step_latitude(
            2, p, lambda at: window[at], weights, ends, coef
        )


def pack(kernel, outs, operands, copies, name):
    return pl.pallas_call(
        kernel,
        out_shape=outs,
        in_specs=[ANY] * operands,
        out_specs=ANY if isinstance(outs, jax.ShapeDtypeStruct) else (ANY,) * len(outs),
        scratch_shapes=[pltpu.SemaphoreType.DMA((copies,))],
        compiler_params=pltpu.CompilerParams(vmem_limit_bytes=40 * 1024 * 1024),
        cost_estimate=pl.CostEstimate(flops=0, bytes_accessed=2**10, transcendentals=0),
        name=name,
    )


def call(kernel, outs, in_specs, out_specs, scratch, flops, name):
    return pl.pallas_call(
        kernel,
        out_shape=outs,
        in_specs=in_specs,
        out_specs=out_specs,
        scratch_shapes=scratch,
        compiler_params=pltpu.CompilerParams(vmem_limit_bytes=40 * 1024 * 1024),
        cost_estimate=pl.CostEstimate(flops=flops, bytes_accessed=2**10, transcendentals=0),
        name=name,
    )


def shaped(*dims, dtype=F32):
    return jax.ShapeDtypeStruct(dims, dtype)


def per_device(x_size, z_size, covariance, table, winds, barriers, mix_a, mix_b):
    send = lambda value, move: lax.ppermute(value, AXES, pairs(move, x_size, z_size))
    dma = lambda n: pltpu.SemaphoreType.DMA((n,))

    piece = lambda n: shaped(n, 256, LEV)
    out_0 = pack(pack_first, shaped(256, 512), 1, 1, "pack_first")(covariance)
    pair_0 = send(out_0, swap_y)
    covariance, mix_a, mix_b, out_0 = lax.optimization_barrier((covariance, mix_a, mix_b, out_0))
    out_across, out_near, out_core = pack(
        pack_second, (shaped(6, LEV, LEV), piece(7), shaped(2, LEV, LEV)), 3, 11, "pack_second"
    )(covariance, mix_a, mix_b)
    across = send(out_across, functools.partial(mats_across, x_size))
    near = send(out_near, near_z)
    covariance, out_across = lax.optimization_barrier((covariance, out_across))
    out_1 = pack(pack_swap, shaped(256, 512), 1, 1, "pack_swap")(covariance)
    pair_1 = send(out_1, swap_y)
    out_far_0 = pack(pack_far, piece(4), 2, 5, "pack_far")(pair_0, across)
    far_0 = send(out_far_0, far_z)
    out_far_1 = pack(pack_halo, piece(3), 1, 3, "pack_halo")(pair_1)

    weight = shaped(8, 256, 256, dtype=BF16)
    ends = shaped(4, 256, 256, dtype=BF16)
    prep_scratch = [pltpu.SMEM((2, 16), F32)]
    weights_b, coef_b = call(
        prepare_b, (weight, shaped(144)), [SMEM] * 3 + [VMEM] * 2, (VMEM, SMEM), prep_scratch, 10**3,
        "prepare_b",
    )(table, winds, barriers, across, mix_b)
    far_1 = send(out_far_1, far_z)
    weights_b, far_0, out_far_1 = lax.optimization_barrier((weights_b, far_0, out_far_1))
    block = shaped(2, 512, LEV)
    field = pltpu.VMEM((WINDOW, 256, LEV), F32)
    kept_0, sent_0, ends_b = call(
        functools.partial(sweep_b, 0), (block, block, ends), [SMEM] + [VMEM] * 5, (VMEM,) * 3,
        [field, field], COST, "sweep_b0",
    )(coef_b, weights_b, covariance, pair_0, near, far_0)
    got_0 = send(sent_0, swap_y)
    kept_1, sent_1, out_same, out_cross = call(
        functools.partial(sweep_b, 1), (block, block, shaped(3, 512, LEV), shaped(3, 512, LEV)),
        [SMEM] + [VMEM] * 6 + [ANY, ANY], (VMEM, VMEM, ANY, ANY),
        [field, field, dma(4)], COST, "sweep_b1",
    )(coef_b, weights_b, covariance, pair_1, near, far_1, ends_b, kept_0, sent_0)
    got_1 = send(sent_1, swap_y)
    cross = send(out_cross, halo_cross)
    out_same, out_core, got_0 = lax.optimization_barrier((out_same, out_core, got_0))
    same = send(out_same, halo_same)
    core = send(out_core, mats_core)
    weights_a, ends_a, coef_a = call(
        prepare_a, (weight, ends, shaped(144)), [SMEM] * 3 + [VMEM] * 3, (VMEM, VMEM, SMEM),
        prep_scratch, 10**3, "prepare_a",
    )(table, winds, barriers, mix_a, across, core)
    got_0, weights_a = lax.optimization_barrier((got_0, weights_a))
    relay_0 = send(got_0, relay_core)
    relay_1 = send(got_1[1:], relay_core)

    field = pltpu.VMEM((WINDOW, 512, LEV), F32)
    return call(
        sweep_a, shaped(512, 1024), [SMEM] + [VMEM] * 10, VMEM, [field, field],
        4 * 10**3, "sweep_a",
    )(coef_a, weights_a, ends_a, kept_0, kept_1, got_0, got_1, same, cross, relay_0, relay_1)


def solution(mesh):
    placed = (P("row", "col"), P(), P(), P(), P("row", None, None), P("col", None, None))
    return jax.shard_map(
        functools.partial(per_device, mesh.shape["row"] // 4, mesh.shape["col"] // 2),
        mesh=mesh, in_specs=placed, out_specs=P("col", "row"), check_vma=False,
    )
```
